32 devices in a mesh: group: 4 (over y, x), member: 8 (over z, core).
Axes of the slice: x: 2, y: 2, z: 4, core: 2. Of those that a mesh axis runs over, the one named last changes fastest.
Arguments:
- test_points: bfloat16 [32, 3, 1024], P(('group', 'member')), may hold values from 0 to 4
- test_basis: bfloat16 [32, 2, 1024, 256], P(('group', 'member')), may hold values from -0.25 to 0.25
- source_points: bfloat16 [32, 3, 1024], P(('group', 'member')), may hold values from 0 to 4
- source_basis: bfloat16 [32, 2, 1024, 256], P(('group', 'member')), may hold values from -0.1875 to 0.1875
- excitation: bfloat16 [32, 2, 256, 256], P(('group', 'member')), may hold values from -6 to 6
- preconditioner: bfloat16 [32, 256, 2, 256], P(('group', 'member')), may hold values from -0.25 to 0.25
- plan: int32 [2, 2], replicated, may hold values from 0 to 31, as said below
- solver_owner: int32 [32, 2, 4], P(('group', 'member')), may hold values from 0 to 7, as said below
Outputs:
- result: float32 [32, 256, 2, 256], P(('group', 'member'))
The draws below stay inside these ranges and needn't reach their ends.
Inputs may be any that keep to these rules, and one draw needn't show every extreme that they name: `plan`: distinct domain indices. `solver_owner`: owners lie in the tile's own group. At most 2 of one device's 8 tiles go to one owner; in every group one owner takes exactly 2 tiles from every device of the group.
All inputs are finite; a program needn't handle non-finite values.
Results may differ from the reference program's by a relative error of at most 0.008.
Values may be sent and summed in bfloat16 or wider, within the bound.
No kernel may reach another device: no remote copies, remote signals or barrier semaphores. Data moves between devices by JAX's collectives and lax.ppermute only.
A program may use at most 128 MiB of HBM per device.

```python
import math
import jax
import jax.numpy as jnp
from jax import lax

NB = 256
EXC = 256
SRC_PTS = 1024
TEST_DEV = 1024
DOM_DEV = 2
DOM_PTS = 512
ROUNDS = 2
PER_ROUND = 2
DOMAINS = 32
N_MEMBER = 8


def draw_plan(key, part):
    inner = jax.random.permutation(jax.random.fold_in(key, 11), DOMAINS - 2) + 1
    ends = jnp.array([0, DOMAINS - 1], dtype=jnp.int32)
    picked = jnp.concatenate([ends, inner[:ROUNDS * PER_ROUND - 2].astype(jnp.int32)])
    order = jax.random.permutation(jax.random.fold_in(key, 12), ROUNDS * PER_ROUND)
    return picked[order].reshape(ROUNDS, PER_ROUND).astype(jnp.int32)


def draw_solver_owner(key, part):
    tile_count = DOM_DEV * ROUNDS * PER_ROUND
    groups = DOMAINS // N_MEMBER
    hottest = jax.random.randint(jax.random.fold_in(key, 21), (groups,), 0, N_MEMBER)
    hot_each = jnp.repeat(hottest, N_MEMBER)

    def one_domain(subkey, hot_member):
        key_one, key_two, key_three = jax.random.split(subkey, 3)
        others = (hot_member + 1 + jax.random.permutation(key_one, N_MEMBER - 1)) % N_MEMBER
        paired = jax.random.randint(key_two, (), 0, 2)
        head = jnp.stack([hot_member, hot_member])
        spread = jnp.concatenate([head, others[:tile_count - 2]])
        doubled = jnp.concatenate([head, jnp.repeat(others[:(tile_count - 2) // 2], 2)])
        picked = jnp.where(paired == 1, doubled, spread)
        order = jax.random.permutation(key_three, tile_count)
        return picked[order]
    keys = jax.random.split(jax.random.fold_in(key, 22), DOMAINS)
    flat = jax.vmap(one_domain)(keys, hot_each)
    return flat.reshape(DOMAINS, DOM_DEV, ROUNDS * PER_ROUND).astype(jnp.int32)


def level_of(rng, dims, cuts, least, high):
    def one(dim, parts):
        draws = jax.random.uniform(jax.random.fold_in(jax.random.fold_in(rng, 6), dim), (parts,), jnp.float32, least / len(cuts), high / len(cuts))
        return jnp.repeat(jnp.exp(draws), dims[dim] // parts).reshape((-1,) + (1,) * (len(dims) - dim - 1))

    loudness = one(*cuts[0])
    for cut in cuts[1:]:
        loudness = loudness * one(*cut)
    return loudness


def normal_values(stream_key, extent, scale, bound, cuts=(), kind=jnp.bfloat16):
    level = level_of(stream_key, extent, cuts, -0.22, 0.18) if cuts else 1.0
    result = jax.random.normal(stream_key, extent, jnp.float32) * scale * level
    return jnp.minimum(jnp.maximum(result, -bound), bound).astype(kind)


def setup_inputs(seed: int = 0) -> dict:
    splits = jax.random.split(jax.random.key(seed), 9)
    test_points = jnp.clip(4.0 * jax.random.uniform(splits[0], (DOMAINS, 3, TEST_DEV), jnp.float32) ** level_of(splits[0], (DOMAINS, 3, TEST_DEV), ((0, 32),), -0.2, 0.2), 0.0, 4.0).astype(jnp.bfloat16)
    test_basis = normal_values(splits[1], (DOMAINS, 2, TEST_DEV, NB), DOM_PTS ** -0.5, 0.25, ((0, 32),))
    source_points = jnp.clip(4.0 * jax.random.uniform(splits[2], (DOMAINS, 3, SRC_PTS), jnp.float32) ** level_of(splits[2], (DOMAINS, 3, SRC_PTS), ((0, 32),), -0.2, 0.2), 0.0, 4.0).astype(jnp.bfloat16)
    source_basis = normal_values(splits[3], (DOMAINS, 2, SRC_PTS, NB), SRC_PTS ** -0.5, 0.1875, ((0, 32),))
    excitation = normal_values(splits[4], (DOMAINS, 2, NB, EXC), 1.0, 6.0, ((0, 32),))
    preconditioner = normal_values(splits[5], (DOMAINS, NB, 2, NB), (2 * NB) ** -0.5, 0.25, ((0, 32),))
    plan = draw_plan(jax.random.fold_in(splits[8], 71), 0)
    solver_owner = draw_solver_owner(jax.random.fold_in(splits[8], 71), 0)
    return {"test_points": test_points, "test_basis": test_basis, "source_points": source_points, "source_basis": source_basis, "excitation": excitation, "preconditioner": preconditioner, "plan": plan, "solver_owner": solver_owner}


wave_number = 2.0 * math.pi
wire_radius = 0.05

def green_parts(points_test, points_source):
    near = points_test.astype(jnp.float32)
    far = points_source.astype(jnp.float32)
    dist_sq = jnp.zeros((near.shape[1], far.shape[1]), jnp.float32)
    for component in range(3):
        offset = near[component][:, None] - far[component][None, :]
        dist_sq = dist_sq + offset * offset
    distance = jnp.sqrt(dist_sq + wire_radius * wire_radius)
    weight = 1.0 / (4.0 * math.pi * distance)
    green_re = (jnp.cos(wave_number * distance) * weight).astype(jnp.bfloat16)
    green_im = (-jnp.sin(wave_number * distance) * weight).astype(jnp.bfloat16)
    return (green_re, green_im)

def product(left, right):
    return jnp.dot(left, right, preferred_element_type=jnp.float32)

def reference(test_points, test_basis, source_points, source_basis, excitation, preconditioner, plan, solver_owner):
    owners = plan.reshape(-1).astype(jnp.int32)
    n_sources = owners.shape[0]
    per_domain = TEST_DEV // DOM_DEV
    far_points = source_points[owners]
    far_basis = source_basis[owners]
    far_coeff = excitation[owners]

    def one_device(index, assembled):
        own_points = test_points[index]
        own_basis = test_basis[index]
        group_base = index // N_MEMBER * N_MEMBER
        for source_slot in range(n_sources):
            green_re, green_im = green_parts(own_points, far_points[source_slot])
            basis_re = far_basis[source_slot, 0]
            basis_im = far_basis[source_slot, 1]
            half_re = (product(green_re, basis_re) - product(green_im, basis_im)).astype(jnp.bfloat16)
            half_im = (product(green_re, basis_im) + product(green_im, basis_re)).astype(jnp.bfloat16)
            coeff_re = far_coeff[source_slot, 0]
            coeff_im = far_coeff[source_slot, 1]
            for domain in range(DOM_DEV):
                start = domain * per_domain
                test_re = own_basis[0, start:start + per_domain]
                test_im = own_basis[1, start:start + per_domain]
                part_re = half_re[start:start + per_domain]
                part_im = half_im[start:start + per_domain]
                tile_re = (product(test_re.T, part_re) + product(test_im.T, part_im)).astype(jnp.bfloat16)
                tile_im = (product(test_re.T, part_im) - product(test_im.T, part_re)).astype(jnp.bfloat16)
                out_re = product(tile_re, coeff_re) - product(tile_im, coeff_im)
                out_im = product(tile_re, coeff_im) + product(tile_im, coeff_re)
                target = (group_base + solver_owner[index, domain, source_slot]).astype(jnp.int32)
                assembled = assembled.at[target].add(jnp.concatenate([out_re, out_im], axis=1))
        return assembled
    start_sum = jnp.zeros((DOMAINS, NB, 2 * EXC), jnp.float32)
    assembled = lax.fori_loop(0, DOMAINS, one_device, start_sum)
    assembled_low = assembled.astype(jnp.bfloat16)
    z_re = assembled_low[:, :, :EXC].astype(jnp.float32)
    z_im = assembled_low[:, :, EXC:].astype(jnp.float32)
    inv_re = preconditioner[:, :, 0, :].astype(jnp.float32)
    inv_im = preconditioner[:, :, 1, :].astype(jnp.float32)
    res_re = jnp.einsum('obk,oke->obe', inv_re, z_re) - jnp.einsum('obk,oke->obe', inv_im, z_im)
    res_im = jnp.einsum('obk,oke->obe', inv_re, z_im) + jnp.einsum('obk,oke->obe', inv_im, z_re)
    return jnp.stack([res_re, res_im], axis=2)
```

```python
import functools
import math

import jax
import jax.numpy as jnp
import numpy as np
from jax import lax
from jax.experimental import pallas as pl
from jax.experimental.pallas import tpu as pltpu
from jax.sharding import Mesh
from jax.sharding import PartitionSpec as P

CORES = 2
BLOCK = 256
PIECES = 2
FEATURES = 32
MIB = 2**20

wire_radius = 0.05
middle = 2.0
green_scale = 1.0 / (4.0 * math.pi)

COS_TERMS = (
    0.9999992215563883,
    -19.738982513245205,
    64.9287265171896,
    -85.27239586454552,
    58.794033467936565,
    -21.076773714433187,
)
SIN_TERMS = (
    6.283055796101308,
    -41.331214171938136,
    81.36681334731878,
    -74.47799414788796,
    32.78138228313484,
)

SHARE = 2 * CORES
COORDS = 3
CHIPS = ("group", "z")
EVERY = ("group", "z", "core")


def dot(left, right):
    return jnp.dot(left, right, preferred_element_type=jnp.float32)


def horner(value, terms):
    total = jnp.float32(terms[-1])
    for term in terms[-2::-1]:
        total = total * value + jnp.float32(term)
    return total


def green_pair(dist_sq):
    inverse = lax.rsqrt(dist_sq)
    distance = dist_sq * inverse
    turn = distance - jnp.round(distance)
    square = turn * turn
    real = horner(square, [green_scale * c for c in COS_TERMS]) * inverse
    imag = horner(square, [-green_scale * c for c in SIN_TERMS]) * (turn * inverse)
    return real.astype(jnp.bfloat16), imag.astype(jnp.bfloat16)


def split_terms(value, count):
    parts = []
    for _ in range(count):
        part = rounded(value)
        parts.append(part)
        value = value - part
    return parts


def point_terms(coords):
    high, low = split_terms(coords.astype(jnp.float32) - middle, 2)
    exact = high + low
    return high, low, jnp.sum(exact * exact, axis=0, keepdims=True)


def rounded(value):
    return value.astype(jnp.bfloat16).astype(jnp.float32)


def near_features(points):
    high, low, norm = point_terms(points)
    one = jnp.ones_like(norm)
    rows = split_terms(norm, 3) + [one, one, one]
    rows += [-2.0 * high, -2.0 * high, -2.0 * low, -2.0 * low]
    used = 6 + 4 * points.shape[0]
    rows.append(jnp.zeros((FEATURES - used, points.shape[1]), jnp.float32))
    return jnp.concatenate(rows, axis=0)


def far_features(points):
    high, low, norm = point_terms(points)
    norm = norm + jnp.float32(wire_radius * wire_radius)
    one = jnp.ones_like(norm)
    rows = [one, one, one] + split_terms(norm, 3)
    rows += [high, low, high, low]
    used = 6 + 4 * points.shape[0]
    rows.append(jnp.zeros((FEATURES - used, points.shape[1]), jnp.float32))
    return jnp.concatenate(rows, axis=0).astype(jnp.bfloat16)


def params(mib):
    return pltpu.CompilerParams(vmem_limit_bytes=mib * MIB)


TOKEN = jax.ShapeDtypeStruct((8, 128), jnp.float32)
SMALL = pl.CostEstimate(flops=1, bytes_accessed=1, transcendentals=0)


def whole(count):
    return [pl.BlockSpec(memory_space=pltpu.VMEM)] * count


def scalars(count):
    return [pl.BlockSpec(memory_space=pltpu.SMEM)] * count


def slot_place(slot, depths, info_ref, plan_ref):
    per_round = plan_ref.shape[1]
    owner = plan_ref[slot // per_round, slot % per_round]
    chip = owner // CORES
    return (chip // depths) ^ info_ref[1], (chip % depths) ^ info_ref[2], (owner % CORES) ^ info_ref[0]


def fold_kernel(core_ref, basis_ref, coeff_ref, keep_ref, send_ref):
    rows, cols = keep_ref.shape
    half = cols // 2
    right = jnp.concatenate([coeff_ref[0], coeff_ref[1]], axis=1)
    for turned, out_ref in ((1, send_ref), (0, keep_ref)):
        first = pl.multiple_of((core_ref[0] ^ turned) * rows, rows)
        upper = dot(basis_ref[0, pl.ds(first, rows)], right)
        lower = dot(basis_ref[1, pl.ds(first, rows)], right)
        out_ref[:, :half] = (upper[:, :half] - lower[:, half:]).astype(jnp.bfloat16)
        out_ref[:, half:] = (upper[:, half:] + lower[:, :half]).astype(jnp.bfloat16)


def fold(core, basis, coeff):
    points, n_basis = basis.shape[1:]
    n_excite = coeff.shape[2]
    shape = jax.ShapeDtypeStruct((points // CORES, 2 * n_excite), jnp.bfloat16)
    return pl.pallas_call(
        fold_kernel,
        in_specs=scalars(1) + whole(2),
        out_specs=whole(2),
        out_shape=[shape, shape],
        compiler_params=params(12),
        cost_estimate=SMALL,
    )(core, basis, coeff)


def pack(points):
    def kernel(*refs):
        *ins, out_ref = refs
        for place, in_ref in enumerate(ins):
            out_ref[place] = in_ref[...]

    return pl.pallas_call(
        kernel,
        out_shape=jax.ShapeDtypeStruct((len(points),) + points[0].shape, points[0].dtype),
        compiler_params=params(4),
        cost_estimate=SMALL,
    )(*points)


def spread(points, chips, depths):
    width = points.shape[1] // SHARE

    def kernel(points_ref, out_ref):
        for device in range(chips * CORES):
            place = (device % CORES) * 2 + (device // CORES) % depths % 2
            out_ref[device] = points_ref[:, place * width : (place + 1) * width]

    return pl.pallas_call(
        kernel,
        out_shape=jax.ShapeDtypeStruct((chips * CORES, points.shape[0], width), points.dtype),
        compiler_params=params(4),
        cost_estimate=SMALL,
    )(points)


def planned_features(plan, points):
    n_sources, width = plan.size, points.shape[2]

    def kernel(plan_ref, points_ref, out_ref):
        for slot in range(n_sources):
            owner = plan_ref[slot // plan.shape[1], slot % plan.shape[1]]
            out_ref[:, slot * width : (slot + 1) * width] = far_features(points_ref[owner])

    return pl.pallas_call(
        kernel,
        in_specs=scalars(1) + whole(1),
        out_specs=pl.BlockSpec(memory_space=pltpu.VMEM),
        out_shape=jax.ShapeDtypeStruct((FEATURES, n_sources * width), jnp.bfloat16),
        compiler_params=params(4),
        cost_estimate=SMALL,
    )(plan, points)


def primary_kernel(depths, info_ref, plan_ref, keep_ref, other_ref, *out_refs):
    core, group, depth = info_ref[0], info_ref[1], info_ref[2]
    first = (group * depths + depth) * CORES
    *out_refs, twin_ref = out_refs
    owners = [plan_ref[i, j] for i in range(plan_ref.shape[0]) for j in range(plan_ref.shape[1])]
    planned = jnp.int32(0)
    twin = jnp.int32(0)
    for place, owner in enumerate(owners):
        planned = planned | (owner == first).astype(jnp.int32)
        for other in owners[:place]:
            twin = twin | (owner // CORES == other // CORES).astype(jnp.int32)
    twin_ref[0] = twin
    own = planned ^ core
    for step, out_ref in enumerate(out_refs):
        for parity in range(2):
            span = slice(parity * (depths // 2), (parity + 1) * (depths // 2))

            @pl.when(own == 1)
            def _():
                out_ref[span] = keep_ref[parity, group ^ step]

            @pl.when(own == 0)
            def _():
                out_ref[span] = other_ref[parity, group ^ step]


def primary_parts(info, plan, depths, keep, other):
    _, count, _, per, cols = keep.shape
    shape = jax.ShapeDtypeStruct((depths, per, cols), keep.dtype)
    return pl.pallas_call(
        functools.partial(primary_kernel, depths),
        in_specs=scalars(2) + whole(2),
        out_specs=whole(count) + scalars(1),
        out_shape=[shape] * count + [jax.ShapeDtypeStruct((1,), jnp.int32)],
        compiler_params=params(6),
        cost_estimate=SMALL,
    )(info, plan, keep, other)


def regroup(info, parts, depths):
    n_groups = len(parts)
    shape = jax.ShapeDtypeStruct((n_groups,) + parts[0].shape[1:], parts[0].dtype)

    def kernel(info_ref, *refs):
        ins, outs, token_ref = refs[:n_groups], refs[n_groups:-1], refs[-1]
        token_ref[...] = jnp.zeros_like(token_ref)
        for step, out_ref in enumerate(outs):
            to = info_ref[2] ^ step
            for place, in_ref in enumerate(ins):
                out_ref[place] = in_ref[(to & 1) * (depths // 2) + (to >> 1)]

    return pl.pallas_call(
        kernel,
        in_specs=scalars(1) + whole(n_groups),
        out_specs=whole(depths + 1),
        out_shape=[shape] * depths + [TOKEN],
        compiler_params=params(6),
        cost_estimate=SMALL,
    )(info, *parts)


def pick(info, plan, second, arrived):
    n_sources, depths = plan.size, len(arrived)
    shape = jax.ShapeDtypeStruct((n_sources,) + arrived[0].shape[1:], arrived[0].dtype)

    def kernel(info_ref, plan_ref, second_ref, *refs):
        *ins, out_ref, sem = refs
        owners = [plan_ref[divmod(slot, plan.shape[1])] for slot in range(n_sources)]
        for slot in range(n_sources):
            across, along, _ = slot_place(slot, depths, info_ref, plan_ref)
            for step, in_ref in enumerate(ins):

                @pl.when(along == step)
                def _():
                    out_ref[slot] = in_ref[across]

            after = jnp.int32(0)
            for owner in owners:
                after = after | (owner == owners[slot] - 1).astype(jnp.int32)

            @pl.when((owners[slot] % CORES == 1) & (after == 1))
            def _():
                copy = pltpu.make_async_copy(
                    second_ref.at[owners[slot] // CORES], out_ref.at[slot], sem
                )
                copy.start()
                copy.wait()

    return pl.pallas_call(
        kernel,
        in_specs=scalars(2) + [pl.BlockSpec(memory_space=pl.ANY)] + whole(depths),
        out_specs=pl.BlockSpec(memory_space=pltpu.VMEM),
        out_shape=shape,
        scratch_shapes=[pltpu.SemaphoreType.DMA],
        compiler_params=params(6),
        cost_estimate=SMALL,
    )(info, plan, second, *arrived)


def prepare_kernel(place, points_ref, *refs):
    *basis_refs, near_ref, left_ref = refs
    n_domains = left_ref.shape[0]
    rows = basis_refs[0].shape[1] // n_domains
    n_basis = basis_refs[0].shape[2]
    near_ref[...] = near_features(points_ref[place, :COORDS]).T.astype(jnp.bfloat16)
    for domain in range(n_domains):
        span = slice(domain * rows, (domain + 1) * rows)
        real = basis_refs[0][0, span].T
        imag = basis_refs[-1][basis_refs[-1].shape[0] - 1, span].T
        left_ref[domain, :n_basis, :rows] = real
        left_ref[domain, :n_basis, rows:] = imag
        left_ref[domain, n_basis:, :rows] = -imag
        left_ref[domain, n_basis:, rows:] = real


def prepare(place, points, basis, n_domains):
    _, rows, n_basis = basis[0].shape
    return pl.pallas_call(
        functools.partial(prepare_kernel, place),
        out_shape=[
            jax.ShapeDtypeStruct((rows, FEATURES), jnp.bfloat16),
            jax.ShapeDtypeStruct((n_domains, 2 * n_basis, 2 * rows // n_domains), jnp.bfloat16),
        ],
        compiler_params=params(8),
        cost_estimate=SMALL,
    )(points, *basis)


def tested_kernel(n_devices, far_ref, *refs):
    nears, lefts, outs = (refs[i * n_devices : (i + 1) * n_devices] for i in range(3))
    token_ref, *green = refs[3 * n_devices :]
    token_ref[...] = jnp.zeros_like(token_ref)
    n_domains, size, _ = lefts[0].shape
    rows = nears[0].shape[0] // n_domains
    n_basis = size // 2
    blocks = far_ref.shape[1] // BLOCK
    work = [(i, d, b) for i in range(n_devices) for d in range(n_domains) for b in range(blocks)]

    def interact(index, piece):
        device, domain, block = work[index]
        part = rows // PIECES // 2
        span = slice(block * BLOCK, (block + 1) * BLOCK)
        into = green[index % 2]
        for first in range(2 * piece * part, 2 * (piece + 1) * part, part):
            near = nears[device][domain * rows + first : domain * rows + first + part]
            real, imag = green_pair(dot(near, far_ref[:, span]))
            into[first : first + part] = real
            into[rows + first : rows + first + part] = imag

    def test(index, piece):
        device, domain, block = work[index]
        start = (PIECES * block + piece) * BLOCK
        some = slice(piece * n_basis, (piece + 1) * n_basis)
        result = dot(lefts[device][domain, some], green[index % 2][...])
        outs[device][domain, :, start : start + BLOCK] = result.astype(jnp.bfloat16)

    for piece in range(PIECES):
        interact(0, piece)
    for index in range(len(work)):
        for piece in range(PIECES):
            test(index, piece)
            if index + 1 < len(work):
                interact(index + 1, piece)


def tested(far, nears, lefts):
    n_domains, size, twice = lefts[0].shape
    columns = far.shape[1]
    shape = jax.ShapeDtypeStruct((n_domains, size // 2, 2 * columns), jnp.bfloat16)
    return pl.pallas_call(
        functools.partial(tested_kernel, len(nears)),
        out_shape=[shape] * len(nears) + [TOKEN],
        scratch_shapes=[
            pltpu.VMEM((twice, BLOCK), jnp.bfloat16),
            pltpu.VMEM((twice, BLOCK), jnp.bfloat16),
        ],
        compiler_params=params(8),
        cost_estimate=pl.CostEstimate(
            flops=8 * len(nears) * n_domains * size * twice * columns,
            bytes_accessed=4 * MIB,
            transcendentals=0,
        ),
    )(far, *nears, *lefts)


def gather_kernel(n_tests, places, info_ref, *refs):
    owner_ref, tests = refs[0], refs[1 : n_tests + 1]
    *pieces, keep_ref, send_ref, far, total = refs[n_tests + 1 :]
    n_sources, twice, cols = far.shape
    width, half = twice // 2, cols // 2
    n_depth, n_basis, _ = keep_ref.shape
    n_domains = tests[0].shape[0]
    core, group, depth = info_ref[0], info_ref[1], info_ref[2]

    def fill(start, per, value):
        for slot in range(n_sources):
            block = value(slot)
            far[slot, pl.ds(start, per)] = block
            far[slot, pl.ds(width + start, per), :half] = -block[:, half:]
            far[slot, pl.ds(width + start, per), half:] = block[:, :half]

    if places is None:
        fill(0, width, lambda slot: pieces[0][slot])
    else:
        for piece, (across, steps) in zip(pieces, places):
            per = piece.shape[-2]
            for place, along in enumerate(steps):
                chip = (group ^ across) * (n_depth // 2) + ((depth ^ along) >> 1)
                start = pl.multiple_of(chip * per, per)
                fill(start, per, lambda slot: piece[place, slot])
    total[...] = jnp.zeros_like(total)

    def add_domain(domain, carry):
        for place, test in enumerate(tests):
            for slot in range(n_sources):
                left = test[domain, :, slot * twice : (slot + 1) * twice]
                owner = owner_ref[place, domain * n_sources + slot]
                total[owner] += dot(left, far[slot])
        return carry

    lax.fori_loop(0, n_domains, add_domain, 0)
    for step in range(n_depth):
        owner = CORES * (depth ^ step) + core
        keep_ref[step] = total[owner]
        send_ref[step] = total[owner ^ 1].astype(jnp.bfloat16)


def gather_products(info, owners, tests, pieces, places, depths, n_sources):
    n_domains, n_basis, columns = tests[0].shape
    cols = pieces[0].shape[-1]
    shape = (depths, n_basis, cols)
    return pl.pallas_call(
        functools.partial(gather_kernel, len(tests), places),
        in_specs=scalars(2) + whole(len(tests) + len(pieces)),
        out_specs=whole(2),
        out_shape=[
            jax.ShapeDtypeStruct(shape, jnp.float32),
            jax.ShapeDtypeStruct(shape, jnp.bfloat16),
        ],
        scratch_shapes=[
            pltpu.VMEM((n_sources, columns // n_sources, cols), jnp.bfloat16),
            pltpu.VMEM((CORES * depths, n_basis, cols), jnp.float32),
        ],
        compiler_params=params(14),
        cost_estimate=pl.CostEstimate(
            flops=2 * len(tests) * n_domains * n_basis * columns * cols,
            bytes_accessed=MIB,
            transcendentals=0,
        ),
    )(info, owners, *tests, *pieces)


def finish_kernel(inverse_ref, keep_ref, *refs):
    *others, out_ref = refs
    half = keep_ref.shape[2] // 2
    summed = keep_ref[0]
    for other in others:
        summed = summed + other[...].astype(jnp.float32)
    low = summed.astype(jnp.bfloat16)
    upper = dot(inverse_ref[:, : low.shape[0]], low)
    lower = dot(inverse_ref[:, low.shape[0] :], low)
    out_ref[:, 0] = upper[:, :half] - lower[:, half:]
    out_ref[:, 1] = upper[:, half:] + lower[:, :half]


def finish(inverse, keep, others):
    _, rows, cols = keep.shape
    return pl.pallas_call(
        finish_kernel,
        out_shape=jax.ShapeDtypeStruct((rows, 2, cols // 2), jnp.float32),
        compiler_params=params(12),
    )(inverse, keep, *others)


def partner(value, axis, step, size):
    return lax.ppermute(value, axis, [(i, i ^ step) for i in range(size)])


def shards(
    test_points,
    test_basis,
    source_points,
    source_basis,
    excitation,
    preconditioner,
    plan,
    solver_owner,
):
    groups, depths = lax.axis_size("group"), lax.axis_size("z")
    group, depth, core = lax.axis_index("group"), lax.axis_index("z"), lax.axis_index("core")
    chips = groups * depths
    n_domains, n_sources = solver_owner.shape[1:]
    src_points = source_points.shape[2]
    n_excite = excitation.shape[3]
    width = src_points // SHARE
    per = CORES * width // chips
    cols = 2 * n_excite
    info = jnp.stack([core, group, depth, depths]).astype(jnp.int32)
    def sibling(value):
        return partner(value, "core", 1, CORES)

    bases = [test_basis[0], sibling(test_basis[0]), partner(test_basis[0], "z", 1, depths)]

    keep, send = fold(info, source_basis[0], excitation[0])
    other = sibling(send)
    cut = (2, groups, depths // 2, per, cols)
    *parts, twin = primary_parts(info, plan, depths, keep.reshape(cut), other.reshape(cut))

    def rest_of_second(keep, other):
        first_planned = jnp.any(plan == (group * depths + depth) * CORES)
        rest = jnp.where(first_planned == (core == 0), other, keep).reshape(cut)
        rest = rest.transpose(1, 2, 0, 3, 4).reshape(chips, per, cols)
        return lax.all_to_all(rest, CHIPS, 0, 0, tiled=True)

    second = lax.cond(
        twin[0] > 0, rest_of_second, lambda _, other: other.reshape(chips, per, cols), keep, other
    )
    parts, source_points, test_points, solver_owner = lax.optimization_barrier(
        (parts, source_points, test_points, solver_owner)
    )
    parts = [parts[0]] + [partner(parts[k], "group", k, groups) for k in range(1, groups)]

    far_points = lax.all_to_all(spread(source_points[0], chips, depths), EVERY, 0, 0, tiled=True)
    n_tiles = n_domains * n_sources
    owner_row = solver_owner[0].reshape(1, n_tiles).astype(test_points.dtype)
    owner_row = jnp.pad(owner_row, ((0, 0), (0, src_points - n_tiles)))
    sides = jnp.concatenate([test_points[0], owner_row], axis=0)
    sides = pack((sides, sibling(sides)))

    parts, bases[2], sides = lax.optimization_barrier((parts, bases[2], sides))
    bases.append(sibling(bases[2]))
    *arrived, token = regroup(info, parts, depths)
    token, sides, far_points = lax.optimization_barrier((token, sides, far_points))
    packs = [sides, partner(sides, "z", 1, depths)]
    tile_owners = jnp.concatenate([side[:, COORDS, :n_tiles] for side in packs]).astype(jnp.int32)
    arrived = [arrived[0]] + [partner(arrived[k], "z", k, depths) for k in range(1, depths)]

    far = planned_features(plan, far_points)

    def test(place):
        near, left = prepare(
            place % CORES, packs[place // CORES], [bases[place]], n_domains
        )
        result, token = tested(far, [near], [left])
        tests.append(result)
        return token

    tests = []
    tokens = [test(0), test(1)]
    tokens, arrived = lax.optimization_barrier((tokens, arrived))
    mine = pick(info, plan, second, arrived)

    steps = list(range(0, depths, 2))
    held = jnp.stack([mine] + [partner(mine, "z", k, depths) for k in steps[1:]])
    token, held = lax.optimization_barrier((test(2), held))
    pieces = [held] + [partner(held, "group", k, groups) for k in range(1, groups)]
    places = [(k, steps) for k in range(groups)]
    test(3)
    if per % 16:
        half = depths // 2
        sorted_pieces = [[None] * half for _ in range(groups)]
        for piece, (across, steps) in zip(pieces, places):
            for place, along in enumerate(steps):
                sorted_pieces[across][along // 2] = piece[place]
        stacked = jnp.stack([jnp.stack(row) for row in sorted_pieces])
        stacked = stacked[group ^ jnp.arange(groups)][:, (depth // 2) ^ jnp.arange(half)]
        pieces = [stacked.transpose(2, 0, 1, 3, 4).reshape(n_sources, width, cols)]
        places = None
    inverse = preconditioner[0].reshape(-1, cols)

    keep, send = gather_products(info, tile_owners, tests, pieces, places, depths, n_sources)
    crossed = sibling(send)
    others = [crossed[0]]
    for step in reversed(range(1, depths)):
        low = (keep[step] + crossed[step].astype(jnp.float32)).astype(jnp.bfloat16)
        others.append(partner(low, "z", step, depths))
    return finish(inverse, keep, others)[None]


def solution(mesh):
    groups, members = mesh.devices.shape
    assert members % SHARE == 0
    fine = Mesh(mesh.devices.reshape(groups, members // CORES, CORES), ("group", "z", "core"))
    every = EVERY
    return jax.shard_map(
        shards,
        mesh=fine,
        in_specs=(
            P(every, None, None),
            P(every, None, None, None),
            P(every, None, None),
            P(every, None, None, None),
            P(every, None, None, None),
            P(every, None, None, None),
            P(),
            P(every, None, None),
        ),
        out_specs=P(every, None, None, None),
        check_vma=False,
    )
```

```python
import functools
import math

import jax
import jax.numpy as jnp
import numpy as np
from jax import lax
from jax.experimental import pallas as pl
from jax.experimental.pallas import tpu as pltpu
from jax.sharding import Mesh
from jax.sharding import PartitionSpec as P

CORES = 2
BLOCK = 256
PIECES = 2
FEATURES = 32
MIB = 2**20

wire_radius = 0.05
middle = 2.0
green_scale = 1.0 / (4.0 * math.pi)

COS_TERMS = (
    0.9999992215563883,
    -19.738982513245205,
    64.9287265171896,
    -85.27239586454552,
    58.794033467936565,
    -21.076773714433187,
)
SIN_TERMS = (
    6.283055796101308,
    -41.331214171938136,
    81.36681334731878,
    -74.47799414788796,
    32.78138228313484,
)

SHARE = 2 * CORES
COORDS = 3
CHIPS = ("group", "z")
EVERY = ("group", "z", "core")


def dot(left, right):
    return jnp.dot(left, right, preferred_element_type=jnp.float32)


def horner(value, terms):
    total = jnp.float32(terms[-1])
    for term in terms[-2::-1]:
        total = total * value + jnp.float32(term)
    return total


def green_pair(dist_sq):
    inverse = lax.rsqrt(dist_sq)
    distance = dist_sq * inverse
    turn = distance - jnp.round(distance)
    square = turn * turn
    real = horner(square, [green_scale * c for c in COS_TERMS]) * inverse
    imag = horner(square, [-green_scale * c for c in SIN_TERMS]) * (turn * inverse)
    return real.astype(jnp.bfloat16), imag.astype(jnp.bfloat16)


def split_terms(value, count):
    parts = []
    for _ in range(count):
        part = rounded(value)
        parts.append(part)
        value = value - part
    return parts


def point_terms(coords):
    high, low = split_terms(coords.astype(jnp.float32) - middle, 2)
    exact = high + low
    return high, low, jnp.sum(exact * exact, axis=0, keepdims=True)


def rounded(value):
    return value.astype(jnp.bfloat16).astype(jnp.float32)


def near_features(points):
    high, low, norm = point_terms(points)
    one = jnp.ones_like(norm)
    rows = split_terms(norm, 3) + [one, one, one]
    rows += [-2.0 * high, -2.0 * high, -2.0 * low, -2.0 * low]
    used = 6 + 4 * points.shape[0]
    rows.append(jnp.zeros((FEATURES - used, points.shape[1]), jnp.float32))
    return jnp.concatenate(rows, axis=0)


def far_features(points):
    high, low, norm = point_terms(points)
    norm = norm + jnp.float32(wire_radius * wire_radius)
    one = jnp.ones_like(norm)
    rows = [one, one, one] + split_terms(norm, 3)
    rows += [high, low, high, low]
    used = 6 + 4 * points.shape[0]
    rows.append(jnp.zeros((FEATURES - used, points.shape[1]), jnp.float32))
    return jnp.concatenate(rows, axis=0).astype(jnp.bfloat16)


def params(mib):
    return pltpu.CompilerParams(vmem_limit_bytes=mib * MIB)


TOKEN = jax.ShapeDtypeStruct((8, 128), jnp.float32)
SMALL = pl.CostEstimate(flops=1, bytes_accessed=1, transcendentals=0)


def whole(count):
    return [pl.BlockSpec(memory_space=pltpu.VMEM)] * count


def scalars(count):
    return [pl.BlockSpec(memory_space=pltpu.SMEM)] * count


def slot_place(slot, depths, info_ref, plan_ref):
    per_round = plan_ref.shape[1]
    owner = plan_ref[slot // per_round, slot % per_round]
    chip = owner // CORES
    return (chip // depths) ^ info_ref[1], (chip % depths) ^ info_ref[2], (owner % CORES) ^ info_ref[0]


def fold_kernel(core_ref, basis_ref, coeff_ref, keep_ref, send_ref):
    rows, cols = keep_ref.shape
    half = cols // 2
    right = jnp.concatenate([coeff_ref[0], coeff_ref[1]], axis=1)
    for turned, out_ref in ((1, send_ref), (0, keep_ref)):
        first = pl.multiple_of((core_ref[0] ^ turned) * rows, rows)
        upper = dot(basis_ref[0, pl.ds(first, rows)], right)
        lower = dot(basis_ref[1, pl.ds(first, rows)], right)
        out_ref[:, :half] = (upper[:, :half] - lower[:, half:]).astype(jnp.bfloat16)
        out_ref[:, half:] = (upper[:, half:] + lower[:, :half]).astype(jnp.bfloat16)


def fold(core, basis, coeff):
    points, n_basis = basis.shape[1:]
    n_excite = coeff.shape[2]
    shape = jax.ShapeDtypeStruct((points // CORES, 2 * n_excite), jnp.bfloat16)
    return pl.pallas_call(
        fold_kernel,
        in_specs=scalars(1) + whole(2),
        out_specs=whole(2),
        out_shape=[shape, shape],
        compiler_params=params(12),
        cost_estimate=SMALL,
    )(core, basis, coeff)


def pack(points):
    def kernel(*refs):
        *ins, out_ref = refs
        for place, in_ref in enumerate(ins):
            out_ref[place] = in_ref[...]

    return pl.pallas_call(
        kernel,
        out_shape=jax.ShapeDtypeStruct((len(points),) + points[0].shape, points[0].dtype),
        compiler_params=params(4),
        cost_estimate=SMALL,
    )(*points)


def spread(points, chips, depths):
    width = points.shape[1] // SHARE

    def kernel(points_ref, out_ref):
        for device in range(chips * CORES):
            place = (device % CORES) * 2 + (device // CORES) % depths % 2
            out_ref[device] = points_ref[:, place * width : (place + 1) * width]

    return pl.pallas_call(
        kernel,
        out_shape=jax.ShapeDtypeStruct((chips * CORES, points.shape[0], width), points.dtype),
        compiler_params=params(4),
        cost_estimate=SMALL,
    )(points)


def planned_features(plan, points, after):
    n_sources, width = plan.size, points.shape[2]

    def kernel(plan_ref, points_ref, after_ref, out_ref):
        for slot in range(n_sources):
            owner = plan_ref[slot // plan.shape[1], slot % plan.shape[1]]
            out_ref[:, slot * width : (slot + 1) * width] = far_features(points_ref[owner])

    return pl.pallas_call(
        kernel,
        in_specs=scalars(1) + whole(2),
        out_specs=pl.BlockSpec(memory_space=pltpu.VMEM),
        out_shape=jax.ShapeDtypeStruct((FEATURES, n_sources * width), jnp.bfloat16),
        compiler_params=params(4),
        cost_estimate=SMALL,
    )(plan, points, after)


def primary_kernel(depths, info_ref, plan_ref, keep_ref, other_ref, *out_refs):
    core, group, depth = info_ref[0], info_ref[1], info_ref[2]
    first = (group * depths + depth) * CORES
    *out_refs, twin_ref = out_refs
    owners = [plan_ref[i, j] for i in range(plan_ref.shape[0]) for j in range(plan_ref.shape[1])]
    planned = jnp.int32(0)
    twin = jnp.int32(0)
    for place, owner in enumerate(owners):
        planned = planned | (owner == first).astype(jnp.int32)
        for other in owners[:place]:
            twin = twin | (owner // CORES == other // CORES).astype(jnp.int32)
    twin_ref[0] = twin
    own = planned ^ core
    for step, out_ref in enumerate(out_refs):
        for parity in range(2):
            span = slice(parity * (depths // 2), (parity + 1) * (depths // 2))

            @pl.when(own == 1)
            def _():
                out_ref[span] = keep_ref[parity, group ^ step]

            @pl.when(own == 0)
            def _():
                out_ref[span] = other_ref[parity, group ^ step]


def primary_parts(info, plan, depths, keep, other):
    _, count, _, per, cols = keep.shape
    shape = jax.ShapeDtypeStruct((depths, per, cols), keep.dtype)
    return pl.pallas_call(
        functools.partial(primary_kernel, depths),
        in_specs=scalars(2) + whole(2),
        out_specs=whole(count) + scalars(1),
        out_shape=[shape] * count + [jax.ShapeDtypeStruct((1,), jnp.int32)],
        compiler_params=params(6),
        cost_estimate=SMALL,
    )(info, plan, keep, other)


def regroup(info, parts, depths):
    n_groups = len(parts)
    shape = jax.ShapeDtypeStruct((n_groups,) + parts[0].shape[1:], parts[0].dtype)

    def kernel(info_ref, *refs):
        ins, outs, token_ref = refs[:n_groups], refs[n_groups:-1], refs[-1]
        token_ref[...] = jnp.zeros_like(token_ref)
        for step, out_ref in enumerate(outs):
            to = info_ref[2] ^ step
            for place, in_ref in enumerate(ins):
                out_ref[place] = in_ref[(to & 1) * (depths // 2) + (to >> 1)]

    return pl.pallas_call(
        kernel,
        in_specs=scalars(1) + whole(n_groups),
        out_specs=whole(depths + 1),
        out_shape=[shape] * depths + [TOKEN],
        compiler_params=params(6),
        cost_estimate=SMALL,
    )(info, *parts)


def pick(info, plan, second, arrived):
    n_sources, depths = plan.size, len(arrived)
    shape = jax.ShapeDtypeStruct((n_sources,) + arrived[0].shape[1:], arrived[0].dtype)

    def kernel(info_ref, plan_ref, second_ref, *refs):
        *ins, out_ref, token_ref, sem = refs
        token_ref[...] = jnp.zeros_like(token_ref)
        owners = [plan_ref[divmod(slot, plan.shape[1])] for slot in range(n_sources)]
        for slot in range(n_sources):
            across, along, _ = slot_place(slot, depths, info_ref, plan_ref)
            before = jnp.int32(0)
            for owner in owners:
                before = before | (owner == owners[slot] - 1).astype(jnp.int32)
            is_second = (owners[slot] % CORES) * before == 1
            for step, in_ref in enumerate(ins):

                @pl.when((along == step) & jnp.logical_not(is_second))
                def _():
                    out_ref[slot] = in_ref[across]

            @pl.when(is_second)
            def _():
                copy = pltpu.make_async_copy(
                    second_ref.at[owners[slot] // CORES], out_ref.at[slot], sem
                )
                copy.start()
                copy.wait()

    return pl.pallas_call(
        kernel,
        in_specs=scalars(2) + [pl.BlockSpec(memory_space=pl.ANY)] + whole(depths),
        out_specs=whole(2),
        out_shape=[shape, TOKEN],
        scratch_shapes=[pltpu.SemaphoreType.DMA],
        compiler_params=params(6),
        cost_estimate=SMALL,
    )(info, plan, second, *arrived)


def hold(pieces):
    def kernel(*refs):
        *ins, out_ref, token_ref = refs
        token_ref[...] = jnp.zeros_like(token_ref)
        for place, in_ref in enumerate(ins):
            out_ref[place] = in_ref[...]

    shape = jax.ShapeDtypeStruct((len(pieces),) + pieces[0].shape, pieces[0].dtype)
    return pl.pallas_call(
        kernel, out_shape=[shape, TOKEN], compiler_params=params(6), cost_estimate=SMALL
    )(*pieces)


def prepare_kernel(place, points_ref, *refs):
    *basis_refs, near_ref, left_ref = refs
    n_domains = left_ref.shape[0]
    rows = basis_refs[0].shape[1] // n_domains
    n_basis = basis_refs[0].shape[2]
    near_ref[...] = near_features(points_ref[place, :COORDS]).T.astype(jnp.bfloat16)
    for domain in range(n_domains):
        span = slice(domain * rows, (domain + 1) * rows)
        real = basis_refs[0][0, span].T
        imag = basis_refs[-1][basis_refs[-1].shape[0] - 1, span].T
        left_ref[domain, :n_basis, :rows] = real
        left_ref[domain, :n_basis, rows:] = imag
        left_ref[domain, n_basis:, :rows] = -imag
        left_ref[domain, n_basis:, rows:] = real


def prepare(place, points, basis, n_domains):
    _, rows, n_basis = basis[0].shape
    return pl.pallas_call(
        functools.partial(prepare_kernel, place),
        out_shape=[
            jax.ShapeDtypeStruct((rows, FEATURES), jnp.bfloat16),
            jax.ShapeDtypeStruct((n_domains, 2 * n_basis, 2 * rows // n_domains), jnp.bfloat16),
        ],
        compiler_params=params(8),
        cost_estimate=SMALL,
    )(points, *basis)


def tested_kernel(n_devices, n_after, far_ref, *refs):
    refs = refs[n_after:]
    nears, lefts, outs = (refs[i * n_devices : (i + 1) * n_devices] for i in range(3))
    token_ref, *green = refs[3 * n_devices :]
    token_ref[...] = jnp.zeros_like(token_ref)
    n_domains, size, _ = lefts[0].shape
    rows = nears[0].shape[0] // n_domains
    n_basis = size // 2
    blocks = far_ref.shape[1] // BLOCK
    work = [(i, d, b) for i in range(n_devices) for d in range(n_domains) for b in range(blocks)]

    def interact(index, piece):
        device, domain, block = work[index]
        part = rows // PIECES // 2
        span = slice(block * BLOCK, (block + 1) * BLOCK)
        into = green[index % 2]
        for first in range(2 * piece * part, 2 * (piece + 1) * part, part):
            near = nears[device][domain * rows + first : domain * rows + first + part]
            real, imag = green_pair(dot(near, far_ref[:, span]))
            into[first : first + part] = real
            into[rows + first : rows + first + part] = imag

    def test(index, piece):
        device, domain, block = work[index]
        start = (PIECES * block + piece) * BLOCK
        some = slice(piece * n_basis, (piece + 1) * n_basis)
        result = dot(lefts[device][domain, some], green[index % 2][...])
        outs[device][domain, :, start : start + BLOCK] = result.astype(jnp.bfloat16)

    for piece in range(PIECES):
        interact(0, piece)
    for index in range(len(work)):
        for piece in range(PIECES):
            test(index, piece)
            if index + 1 < len(work):
                interact(index + 1, piece)


def tested(far, nears, lefts, after):
    n_domains, size, twice = lefts[0].shape
    columns = far.shape[1]
    shape = jax.ShapeDtypeStruct((n_domains, size // 2, 2 * columns), jnp.bfloat16)
    return pl.pallas_call(
        functools.partial(tested_kernel, len(nears), len(after)),
        out_shape=[shape] * len(nears) + [TOKEN],
        scratch_shapes=[
            pltpu.VMEM((twice, BLOCK), jnp.bfloat16),
            pltpu.VMEM((twice, BLOCK), jnp.bfloat16),
        ],
        compiler_params=params(8),
        cost_estimate=pl.CostEstimate(
            flops=8 * len(nears) * n_domains * size * twice * columns,
            bytes_accessed=4 * MIB,
            transcendentals=0,
        ),
    )(far, *after, *nears, *lefts)


def gather_kernel(n_tests, places, info_ref, *refs):
    owner_ref, tests = refs[0], refs[1 : n_tests + 1]
    *pieces, keep_ref, send_ref, far, total = refs[n_tests + 1 :]
    n_sources, twice, cols = far.shape
    width, half = twice // 2, cols // 2
    n_depth, n_basis, _ = keep_ref.shape
    n_domains = tests[0].shape[0]
    core, group, depth = info_ref[0], info_ref[1], info_ref[2]

    def fill(start, per, value):
        for slot in range(n_sources):
            block = value(slot)
            far[slot, pl.ds(start, per)] = block
            far[slot, pl.ds(width + start, per), :half] = -block[:, half:]
            far[slot, pl.ds(width + start, per), half:] = block[:, :half]

    if places is None:
        fill(0, width, lambda slot: pieces[0][slot])
    else:
        for piece, (across, steps) in zip(pieces, places):
            per = piece.shape[-2]
            for place, along in enumerate(steps):
                chip = (group ^ across) * (n_depth // 2) + ((depth ^ along) >> 1)
                start = pl.multiple_of(chip * per, per)
                fill(start, per, lambda slot: piece[place, slot])
    total[...] = jnp.zeros_like(total)

    def add_domain(domain, carry):
        for place, test in enumerate(tests):
            for slot in range(n_sources):
                left = test[domain, :, slot * twice : (slot + 1) * twice]
                owner = owner_ref[place, domain * n_sources + slot]
                total[owner] += dot(left, far[slot])
        return carry

    lax.fori_loop(0, n_domains, add_domain, 0)
    for step in range(n_depth):
        owner = CORES * (depth ^ step) + core
        keep_ref[step] = total[owner]
        send_ref[step] = total[owner ^ 1].astype(jnp.bfloat16)


def gather_products(info, owners, tests, pieces, places, depths, n_sources):
    n_domains, n_basis, columns = tests[0].shape
    cols = pieces[0].shape[-1]
    shape = (depths, n_basis, cols)
    return pl.pallas_call(
        functools.partial(gather_kernel, len(tests), places),
        in_specs=scalars(2) + whole(len(tests) + len(pieces)),
        out_specs=whole(2),
        out_shape=[
            jax.ShapeDtypeStruct(shape, jnp.float32),
            jax.ShapeDtypeStruct(shape, jnp.bfloat16),
        ],
        scratch_shapes=[
            pltpu.VMEM((n_sources, columns // n_sources, cols), jnp.bfloat16),
            pltpu.VMEM((CORES * depths, n_basis, cols), jnp.float32),
        ],
        compiler_params=params(14),
        cost_estimate=pl.CostEstimate(
            flops=2 * len(tests) * n_domains * n_basis * columns * cols,
            bytes_accessed=MIB,
            transcendentals=0,
        ),
    )(info, owners, *tests, *pieces)


def finish_kernel(inverse_ref, keep_ref, *refs):
    *others, out_ref = refs
    half = keep_ref.shape[2] // 2
    summed = keep_ref[0]
    for other in others:
        summed = summed + other[...].astype(jnp.float32)
    low = summed.astype(jnp.bfloat16)
    upper = dot(inverse_ref[:, : low.shape[0]], low)
    lower = dot(inverse_ref[:, low.shape[0] :], low)
    out_ref[:, 0] = upper[:, :half] - lower[:, half:]
    out_ref[:, 1] = upper[:, half:] + lower[:, :half]


def finish(inverse, keep, others):
    _, rows, cols = keep.shape
    return pl.pallas_call(
        finish_kernel,
        out_shape=jax.ShapeDtypeStruct((rows, 2, cols // 2), jnp.float32),
        compiler_params=params(12),
    )(inverse, keep, *others)


def partner(value, axis, step, size):
    return lax.ppermute(value, axis, [(i, i ^ step) for i in range(size)])


def shards(
    test_points,
    test_basis,
    source_points,
    source_basis,
    excitation,
    preconditioner,
    plan,
    solver_owner,
):
    groups, depths = lax.axis_size("group"), lax.axis_size("z")
    group, depth, core = lax.axis_index("group"), lax.axis_index("z"), lax.axis_index("core")
    chips = groups * depths
    n_domains, n_sources = solver_owner.shape[1:]
    src_points = source_points.shape[2]
    n_excite = excitation.shape[3]
    width = src_points // SHARE
    per = CORES * width // chips
    cols = 2 * n_excite
    info = jnp.stack([core, group, depth, depths]).astype(jnp.int32)
    def sibling(value):
        return partner(value, "core", 1, CORES)

    bases = [test_basis[0], sibling(test_basis[0]), partner(test_basis[0], "z", 1, depths)]

    keep, send = fold(info, source_basis[0], excitation[0])
    other = sibling(send)
    cut = (2, groups, depths // 2, per, cols)
    *parts, twin = primary_parts(info, plan, depths, keep.reshape(cut), other.reshape(cut))

    def rest_of_second(keep, other):
        first_planned = jnp.any(plan == (group * depths + depth) * CORES)
        rest = jnp.where(first_planned == (core == 0), other, keep).reshape(cut)
        rest = rest.transpose(1, 2, 0, 3, 4).reshape(chips, per, cols)
        return lax.all_to_all(rest, CHIPS, 0, 0, tiled=True)

    second = lax.cond(
        twin[0] > 0, rest_of_second, lambda _, other: other.reshape(chips, per, cols), keep, other
    )
    parts, source_points, test_points, solver_owner = lax.optimization_barrier(
        (parts, source_points, test_points, solver_owner)
    )
    parts = [parts[0]] + [partner(parts[k], "group", k, groups) for k in range(1, groups)]

    far_points = lax.all_to_all(spread(source_points[0], chips, depths), EVERY, 0, 0, tiled=True)
    n_tiles = n_domains * n_sources
    owner_row = solver_owner[0].reshape(1, n_tiles).astype(test_points.dtype)
    owner_row = jnp.pad(owner_row, ((0, 0), (0, src_points - n_tiles)))
    sides = jnp.concatenate([test_points[0], owner_row], axis=0)
    sides = pack((sides, sibling(sides)))

    parts, bases, sides = lax.optimization_barrier((parts, bases, sides))
    *arrived, token = regroup(info, parts, depths)
    token, far_points = lax.optimization_barrier((token, far_points))
    packs = [sides]
    arrived = [arrived[0]] + [partner(arrived[k], "z", k, depths) for k in range(1, depths)]

    far = planned_features(plan, far_points, token)

    def test(place, *after):
        near, left = prepare(
            place % CORES, packs[place // CORES], [bases[place]], n_domains
        )
        result, _ = tested(far, [near], [left], after)
        tests.append(result)

    tests = []
    test(0)
    mine, token = pick(info, plan, second, arrived)
    packs.append(partner(sides, "z", 1, depths))
    bases.append(sibling(bases[2]))
    tile_owners = jnp.concatenate([side[:, COORDS, :n_tiles] for side in packs]).astype(jnp.int32)
    test(1, token)

    steps = list(range(0, depths, 2))
    held, token = hold([mine] + [partner(mine, "z", k, depths) for k in steps[1:]])
    test(2, token)
    test(3, token)
    pieces = [held] + [partner(held, "group", k, groups) for k in range(1, groups)]
    places = [(k, steps) for k in range(groups)]
    if per % 16:
        half = depths // 2
        sorted_pieces = [[None] * half for _ in range(groups)]
        for piece, (across, steps) in zip(pieces, places):
            for place, along in enumerate(steps):
                sorted_pieces[across][along // 2] = piece[place]
        stacked = jnp.stack([jnp.stack(row) for row in sorted_pieces])
        stacked = stacked[group ^ jnp.arange(groups)][:, (depth // 2) ^ jnp.arange(half)]
        pieces = [stacked.transpose(2, 0, 1, 3, 4).reshape(n_sources, width, cols)]
        places = None
    inverse = preconditioner[0].reshape(-1, cols)

    keep, send = gather_products(info, tile_owners, tests, pieces, places, depths, n_sources)
    crossed = sibling(send)
    others = [crossed[0]]
    for step in reversed(range(1, depths)):
        low = (keep[step] + crossed[step].astype(jnp.float32)).astype(jnp.bfloat16)
        others.append(partner(low, "z", step, depths))
    return finish(inverse, keep, others)[None]


def solution(mesh):
    groups, members = mesh.devices.shape
    assert members % SHARE == 0
    fine = Mesh(mesh.devices.reshape(groups, members // CORES, CORES), ("group", "z", "core"))
    every = EVERY
    return jax.shard_map(
        shards,
        mesh=fine,
        in_specs=(
            P(every, None, None),
            P(every, None, None, None),
            P(every, None, None),
            P(every, None, None, None),
            P(every, None, None, None),
            P(every, None, None, None),
            P(),
            P(every, None, None),
        ),
        out_specs=P(every, None, None, None),
        check_vma=False,
    )
```

```python
import functools
import math

import jax
import jax.numpy as jnp
import numpy as np
from jax import lax
from jax.experimental import pallas as pl
from jax.experimental.pallas import tpu as pltpu
from jax.sharding import Mesh
from jax.sharding import PartitionSpec as P

CORES = 2
BLOCK = 256
PIECES = 2
COLUMNS = 2
FEATURES = 32
MIB = 2**20

wire_radius = 0.05
middle = 2.0
green_scale = 1.0 / (4.0 * math.pi)

COS_TERMS = (
    0.9999992215563883,
    -19.738982513245205,
    64.9287265171896,
    -85.27239586454552,
    58.794033467936565,
    -21.076773714433187,
)
SIN_TERMS = (
    6.283055796101308,
    -41.331214171938136,
    81.36681334731878,
    -74.47799414788796,
    32.78138228313484,
)

SHARE = 2 * CORES
COORDS = 3
CHIPS = ("group", "z")
EVERY = ("group", "z", "core")


def dot(left, right):
    return jnp.dot(left, right, preferred_element_type=jnp.float32)


def horner(value, terms):
    total = jnp.float32(terms[-1])
    for term in terms[-2::-1]:
        total = total * value + jnp.float32(term)
    return total


def green_pair(dist_sq):
    inverse = lax.rsqrt(dist_sq)
    distance = dist_sq * inverse
    turn = distance - jnp.round(distance)
    square = turn * turn
    real = horner(square, [green_scale * c for c in COS_TERMS]) * inverse
    imag = horner(square, [-green_scale * c for c in SIN_TERMS]) * (turn * inverse)
    return real.astype(jnp.bfloat16), imag.astype(jnp.bfloat16)


def split_terms(value, count):
    parts = []
    for _ in range(count):
        part = rounded(value)
        parts.append(part)
        value = value - part
    return parts


def point_terms(coords):
    high, low = split_terms(coords.astype(jnp.float32) - middle, 2)
    exact = high + low
    return high, low, jnp.sum(exact * exact, axis=0, keepdims=True)


def rounded(value):
    return value.astype(jnp.bfloat16).astype(jnp.float32)


def near_features(points):
    high, low, norm = point_terms(points)
    one = jnp.ones_like(norm)
    rows = split_terms(norm, 3) + [one, one, one]
    rows += [-2.0 * high, -2.0 * high, -2.0 * low, -2.0 * low]
    used = 6 + 4 * points.shape[0]
    rows.append(jnp.zeros((FEATURES - used, points.shape[1]), jnp.float32))
    return jnp.concatenate(rows, axis=0)


def far_features(points):
    high, low, norm = point_terms(points)
    norm = norm + jnp.float32(wire_radius * wire_radius)
    one = jnp.ones_like(norm)
    rows = [one, one, one] + split_terms(norm, 3)
    rows += [high, low, high, low]
    used = 6 + 4 * points.shape[0]
    rows.append(jnp.zeros((FEATURES - used, points.shape[1]), jnp.float32))
    return jnp.concatenate(rows, axis=0).astype(jnp.bfloat16)


def params(mib):
    return pltpu.CompilerParams(vmem_limit_bytes=mib * MIB)


TOKEN = jax.ShapeDtypeStruct((8, 128), jnp.float32)
SMALL = pl.CostEstimate(flops=1, bytes_accessed=1, transcendentals=0)


def whole(count):
    return [pl.BlockSpec(memory_space=pltpu.VMEM)] * count


def scalars(count):
    return [pl.BlockSpec(memory_space=pltpu.SMEM)] * count


def slot_place(slot, depths, info_ref, plan_ref):
    per_round = plan_ref.shape[1]
    owner = plan_ref[slot // per_round, slot % per_round]
    chip = owner // CORES
    return (chip // depths) ^ info_ref[1], (chip % depths) ^ info_ref[2], (owner % CORES) ^ info_ref[0]


def fold_kernel(core_ref, basis_ref, coeff_ref, keep_ref, send_ref):
    rows, cols = keep_ref.shape
    half = cols // 2
    right = jnp.concatenate([coeff_ref[0], coeff_ref[1]], axis=1)
    for turned, out_ref in ((1, send_ref), (0, keep_ref)):
        first = pl.multiple_of((core_ref[0] ^ turned) * rows, rows)
        upper = dot(basis_ref[0, pl.ds(first, rows)], right)
        lower = dot(basis_ref[1, pl.ds(first, rows)], right)
        out_ref[:, :half] = (upper[:, :half] - lower[:, half:]).astype(jnp.bfloat16)
        out_ref[:, half:] = (upper[:, half:] + lower[:, :half]).astype(jnp.bfloat16)


def fold(core, basis, coeff):
    points, n_basis = basis.shape[1:]
    n_excite = coeff.shape[2]
    shape = jax.ShapeDtypeStruct((points // CORES, 2 * n_excite), jnp.bfloat16)
    return pl.pallas_call(
        fold_kernel,
        in_specs=scalars(1) + whole(2),
        out_specs=whole(2),
        out_shape=[shape, shape],
        compiler_params=params(12),
        cost_estimate=SMALL,
    )(core, basis, coeff)


def pack(points):
    def kernel(*refs):
        *ins, out_ref = refs
        for place, in_ref in enumerate(ins):
            out_ref[place] = in_ref[...]

    return pl.pallas_call(
        kernel,
        out_shape=jax.ShapeDtypeStruct((len(points),) + points[0].shape, points[0].dtype),
        compiler_params=params(4),
        cost_estimate=SMALL,
    )(*points)


def spread(points, chips, depths):
    width = points.shape[1] // SHARE

    def kernel(points_ref, out_ref):
        for device in range(chips * CORES):
            place = (device % CORES) * 2 + (device // CORES) % depths % 2
            out_ref[device] = points_ref[:, place * width : (place + 1) * width]

    return pl.pallas_call(
        kernel,
        out_shape=jax.ShapeDtypeStruct((chips * CORES, points.shape[0], width), points.dtype),
        compiler_params=params(4),
        cost_estimate=SMALL,
    )(points)


def planned_features(plan, points, after):
    n_sources, width = plan.size, points.shape[2]

    def kernel(plan_ref, points_ref, after_ref, out_ref):
        for slot in range(n_sources):
            owner = plan_ref[slot // plan.shape[1], slot % plan.shape[1]]
            out_ref[:, slot * width : (slot + 1) * width] = far_features(points_ref[owner])

    return pl.pallas_call(
        kernel,
        in_specs=scalars(1) + whole(2),
        out_specs=pl.BlockSpec(memory_space=pltpu.VMEM),
        out_shape=jax.ShapeDtypeStruct((FEATURES, n_sources * width), jnp.bfloat16),
        compiler_params=params(4),
        cost_estimate=SMALL,
    )(plan, points, after)


def primary_kernel(depths, info_ref, plan_ref, keep_ref, other_ref, *out_refs):
    core, group, depth = info_ref[0], info_ref[1], info_ref[2]
    first = (group * depths + depth) * CORES
    *out_refs, twin_ref = out_refs
    owners = [plan_ref[i, j] for i in range(plan_ref.shape[0]) for j in range(plan_ref.shape[1])]
    planned = jnp.int32(0)
    twin = jnp.int32(0)
    for place, owner in enumerate(owners):
        planned = planned | (owner == first).astype(jnp.int32)
        for other in owners[:place]:
            twin = twin | (owner // CORES == other // CORES).astype(jnp.int32)
    twin_ref[0] = twin
    own = planned ^ core
    for step, out_ref in enumerate(out_refs):
        for parity in range(2):
            span = slice(parity * (depths // 2), (parity + 1) * (depths // 2))

            @pl.when(own == 1)
            def _():
                out_ref[span] = keep_ref[parity, group ^ step]

            @pl.when(own == 0)
            def _():
                out_ref[span] = other_ref[parity, group ^ step]


def primary_parts(info, plan, depths, keep, other):
    _, count, _, per, cols = keep.shape
    shape = jax.ShapeDtypeStruct((depths, per, cols), keep.dtype)
    return pl.pallas_call(
        functools.partial(primary_kernel, depths),
        in_specs=scalars(2) + whole(2),
        out_specs=whole(count) + scalars(1),
        out_shape=[shape] * count + [jax.ShapeDtypeStruct((1,), jnp.int32)],
        compiler_params=params(6),
        cost_estimate=SMALL,
    )(info, plan, keep, other)


def regroup(info, parts, depths):
    n_groups = len(parts)
    shape = jax.ShapeDtypeStruct((n_groups,) + parts[0].shape[1:], parts[0].dtype)

    def kernel(info_ref, *refs):
        ins, outs, token_ref = refs[:n_groups], refs[n_groups:-1], refs[-1]
        token_ref[...] = jnp.zeros_like(token_ref)
        for step, out_ref in enumerate(outs):
            to = info_ref[2] ^ step
            for place, in_ref in enumerate(ins):
                out_ref[place] = in_ref[(to & 1) * (depths // 2) + (to >> 1)]

    return pl.pallas_call(
        kernel,
        in_specs=scalars(1) + whole(n_groups),
        out_specs=whole(depths + 1),
        out_shape=[shape] * depths + [TOKEN],
        compiler_params=params(6),
        cost_estimate=SMALL,
    )(info, *parts)


def pick(info, plan, second, arrived):
    n_sources, depths = plan.size, len(arrived)
    shape = jax.ShapeDtypeStruct((n_sources,) + arrived[0].shape[1:], arrived[0].dtype)

    def kernel(info_ref, plan_ref, second_ref, *refs):
        *ins, out_ref, token_ref, sem = refs
        token_ref[...] = jnp.zeros_like(token_ref)
        owners = [plan_ref[divmod(slot, plan.shape[1])] for slot in range(n_sources)]
        for slot in range(n_sources):
            across, along, _ = slot_place(slot, depths, info_ref, plan_ref)
            before = jnp.int32(0)
            for owner in owners:
                before = before | (owner == owners[slot] - 1).astype(jnp.int32)
            is_second = (owners[slot] % CORES) * before == 1
            for step, in_ref in enumerate(ins):

                @pl.when((along == step) & jnp.logical_not(is_second))
                def _():
                    out_ref[slot] = in_ref[across]

            @pl.when(is_second)
            def _():
                copy = pltpu.make_async_copy(
                    second_ref.at[owners[slot] // CORES], out_ref.at[slot], sem
                )
                copy.start()
                copy.wait()

    return pl.pallas_call(
        kernel,
        in_specs=scalars(2) + [pl.BlockSpec(memory_space=pl.ANY)] + whole(depths),
        out_specs=whole(2),
        out_shape=[shape, TOKEN],
        scratch_shapes=[pltpu.SemaphoreType.DMA],
        compiler_params=params(6),
        cost_estimate=SMALL,
    )(info, plan, second, *arrived)


def hold(pieces):
    def kernel(*refs):
        *ins, out_ref, token_ref = refs
        token_ref[...] = jnp.zeros_like(token_ref)
        for place, in_ref in enumerate(ins):
            out_ref[place] = in_ref[...]

    shape = jax.ShapeDtypeStruct((len(pieces),) + pieces[0].shape, pieces[0].dtype)
    return pl.pallas_call(
        kernel, out_shape=[shape, TOKEN], compiler_params=params(6), cost_estimate=SMALL
    )(*pieces)


def prepare_kernel(place, points_ref, *refs):
    *basis_refs, near_ref, left_ref = refs
    n_domains = left_ref.shape[0]
    rows = basis_refs[0].shape[1] // n_domains
    n_basis = basis_refs[0].shape[2]
    near_ref[...] = near_features(points_ref[place, :COORDS]).T.astype(jnp.bfloat16)
    for domain in range(n_domains):
        span = slice(domain * rows, (domain + 1) * rows)
        real = basis_refs[0][0, span].T
        imag = basis_refs[-1][basis_refs[-1].shape[0] - 1, span].T
        left_ref[domain, :n_basis, :rows] = real
        left_ref[domain, :n_basis, rows:] = imag
        left_ref[domain, n_basis:, :rows] = -imag
        left_ref[domain, n_basis:, rows:] = real


def prepare(place, points, basis, n_domains):
    _, rows, n_basis = basis[0].shape
    return pl.pallas_call(
        functools.partial(prepare_kernel, place),
        out_shape=[
            jax.ShapeDtypeStruct((rows, FEATURES), jnp.bfloat16),
            jax.ShapeDtypeStruct((n_domains, 2 * n_basis, 2 * rows // n_domains), jnp.bfloat16),
        ],
        compiler_params=params(8),
        cost_estimate=SMALL,
    )(points, *basis)


def tested_kernel(n_devices, n_after, far_ref, *refs):
    refs = refs[n_after:]
    nears, lefts, outs = (refs[i * n_devices : (i + 1) * n_devices] for i in range(3))
    token_ref, *green = refs[3 * n_devices :]
    token_ref[...] = jnp.zeros_like(token_ref)
    n_domains, size, _ = lefts[0].shape
    rows = nears[0].shape[0] // n_domains
    n_basis = size // 2
    blocks = far_ref.shape[1] // BLOCK
    work = [(i, d, b) for i in range(n_devices) for d in range(n_domains) for b in range(blocks)]

    def interact(index, piece):
        device, domain, block = work[index]
        part = rows // PIECES // 4
        span = slice(block * BLOCK, (block + 1) * BLOCK)
        into = green[index % 2]
        for first in range(4 * piece * part, 4 * (piece + 1) * part, part):
            near = nears[device][domain * rows + first : domain * rows + first + part]
            real, imag = green_pair(dot(near, far_ref[:, span]))
            into[first : first + part] = real
            into[rows + first : rows + first + part] = imag

    def test(index, piece):
        device, domain, block = work[index]
        start = (PIECES * block + piece) * BLOCK
        some = slice(piece * n_basis, (piece + 1) * n_basis)
        result = dot(lefts[device][domain, some], green[index % 2][...])
        outs[device][domain, :, start : start + BLOCK] = result.astype(jnp.bfloat16)

    for piece in range(PIECES):
        interact(0, piece)
    for index in range(len(work)):
        for piece in range(PIECES):
            test(index, piece)
            if index + 1 < len(work):
                interact(index + 1, piece)


def tested(far, nears, lefts, after):
    n_domains, size, twice = lefts[0].shape
    columns = far.shape[1]
    shape = jax.ShapeDtypeStruct((n_domains, size // 2, 2 * columns), jnp.bfloat16)
    return pl.pallas_call(
        functools.partial(tested_kernel, len(nears), len(after)),
        out_shape=[shape] * len(nears) + [TOKEN],
        scratch_shapes=[
            pltpu.VMEM((twice, BLOCK), jnp.bfloat16),
            pltpu.VMEM((twice, BLOCK), jnp.bfloat16),
        ],
        compiler_params=params(8),
        cost_estimate=pl.CostEstimate(
            flops=8 * len(nears) * n_domains * size * twice * columns,
            bytes_accessed=4 * MIB,
            transcendentals=0,
        ),
    )(far, *after, *nears, *lefts)


def gather_kernel(n_tests, places, column, info_ref, *refs):
    owner_ref, tests = refs[0], refs[1 : n_tests + 1]
    *pieces, keep_ref, send_ref, far, total = refs[n_tests + 1 :]
    n_sources, twice, cols = far.shape
    width, half = twice // 2, cols // 2
    n_depth, n_basis, _ = keep_ref.shape
    n_domains = tests[0].shape[0]
    core, group, depth = info_ref[0], info_ref[1], info_ref[2]

    def fill(start, per, value):
        for slot in range(n_sources):
            block = value(slot)
            real = block[:, column * half : (column + 1) * half]
            imag = block[:, (COLUMNS + column) * half : (COLUMNS + column + 1) * half]
            far[slot, pl.ds(start, per), :half] = real
            far[slot, pl.ds(start, per), half:] = imag
            far[slot, pl.ds(width + start, per), :half] = -imag
            far[slot, pl.ds(width + start, per), half:] = real

    if places is None:
        fill(0, width, lambda slot: pieces[0][slot])
    else:
        for piece, (across, steps) in zip(pieces, places):
            per = piece.shape[-2]
            for place, along in enumerate(steps):
                chip = (group ^ across) * (n_depth // 2) + ((depth ^ along) >> 1)
                start = pl.multiple_of(chip * per, per)
                fill(start, per, lambda slot: piece[place, slot])
    total[...] = jnp.zeros_like(total)

    def add_domain(domain, carry):
        for place, test in enumerate(tests):
            for slot in range(n_sources):
                left = test[domain, :, slot * twice : (slot + 1) * twice]
                owner = owner_ref[place, domain * n_sources + slot]
                total[owner] += dot(left, far[slot])
        return carry

    lax.fori_loop(0, n_domains, add_domain, 0)
    for step in range(n_depth):
        owner = CORES * (depth ^ step) + core
        keep_ref[step] = total[owner]
        send_ref[step] = total[owner ^ 1].astype(jnp.bfloat16)


def gather_products(info, owners, tests, pieces, places, depths, n_sources, column):
    n_domains, n_basis, columns = tests[0].shape
    cols = pieces[0].shape[-1] // COLUMNS
    shape = (depths, n_basis, cols)
    return pl.pallas_call(
        functools.partial(gather_kernel, len(tests), places, column),
        in_specs=scalars(2) + whole(len(tests) + len(pieces)),
        out_specs=whole(2),
        out_shape=[
            jax.ShapeDtypeStruct(shape, jnp.float32),
            jax.ShapeDtypeStruct(shape, jnp.bfloat16),
        ],
        scratch_shapes=[
            pltpu.VMEM((n_sources, columns // n_sources, cols), jnp.bfloat16),
            pltpu.VMEM((CORES * depths, n_basis, cols), jnp.float32),
        ],
        compiler_params=params(14),
        cost_estimate=pl.CostEstimate(
            flops=2 * len(tests) * n_domains * n_basis * columns * cols,
            bytes_accessed=MIB,
            transcendentals=0,
        ),
    )(info, owners, *tests, *pieces)


def finish_kernel(inverse_ref, *refs):
    *parts, out_ref = refs
    count = len(parts) // COLUMNS
    for column in range(COLUMNS):
        keep_ref, *others = parts[column * count : (column + 1) * count]
        half = keep_ref.shape[2] // 2
        summed = keep_ref[0]
        for other in others:
            summed = summed + other[...].astype(jnp.float32)
        low = summed.astype(jnp.bfloat16)
        upper = dot(inverse_ref[:, : low.shape[0]], low)
        lower = dot(inverse_ref[:, low.shape[0] :], low)
        span = slice(column * half, (column + 1) * half)
        out_ref[:, 0, span] = upper[:, :half] - lower[:, half:]
        out_ref[:, 1, span] = upper[:, half:] + lower[:, :half]


def finish(inverse, parts):
    rows, cols = inverse.shape
    return pl.pallas_call(
        finish_kernel,
        out_shape=jax.ShapeDtypeStruct((rows, 2, cols // 2), jnp.float32),
        compiler_params=params(12),
    )(inverse, *parts)


def partner(value, axis, step, size):
    return lax.ppermute(value, axis, [(i, i ^ step) for i in range(size)])


def shards(
    test_points,
    test_basis,
    source_points,
    source_basis,
    excitation,
    preconditioner,
    plan,
    solver_owner,
):
    groups, depths = lax.axis_size("group"), lax.axis_size("z")
    group, depth, core = lax.axis_index("group"), lax.axis_index("z"), lax.axis_index("core")
    chips = groups * depths
    n_domains, n_sources = solver_owner.shape[1:]
    src_points = source_points.shape[2]
    n_excite = excitation.shape[3]
    width = src_points // SHARE
    per = CORES * width // chips
    cols = 2 * n_excite
    info = jnp.stack([core, group, depth, depths]).astype(jnp.int32)
    def sibling(value):
        return partner(value, "core", 1, CORES)

    bases = [test_basis[0], sibling(test_basis[0]), partner(test_basis[0], "z", 1, depths)]

    keep, send = fold(info, source_basis[0], excitation[0])
    other = sibling(send)
    cut = (2, groups, depths // 2, per, cols)
    *parts, twin = primary_parts(info, plan, depths, keep.reshape(cut), other.reshape(cut))

    def rest_of_second(keep, other):
        first_planned = jnp.any(plan == (group * depths + depth) * CORES)
        rest = jnp.where(first_planned == (core == 0), other, keep).reshape(cut)
        rest = rest.transpose(1, 2, 0, 3, 4).reshape(chips, per, cols)
        return lax.all_to_all(rest, CHIPS, 0, 0, tiled=True)

    second = lax.cond(
        twin[0] > 0, rest_of_second, lambda _, other: other.reshape(chips, per, cols), keep, other
    )
    parts, source_points, test_points, solver_owner = lax.optimization_barrier(
        (parts, source_points, test_points, solver_owner)
    )
    parts = [parts[0]] + [partner(parts[k], "group", k, groups) for k in range(1, groups)]

    far_points = lax.all_to_all(spread(source_points[0], chips, depths), EVERY, 0, 0, tiled=True)
    n_tiles = n_domains * n_sources
    owner_row = solver_owner[0].reshape(1, n_tiles).astype(test_points.dtype)
    owner_row = jnp.pad(owner_row, ((0, 0), (0, src_points - n_tiles)))
    sides = jnp.concatenate([test_points[0], owner_row], axis=0)
    sides = pack((sides, sibling(sides)))

    parts, bases, sides = lax.optimization_barrier((parts, bases, sides))
    *arrived, token = regroup(info, parts, depths)
    token, far_points = lax.optimization_barrier((token, far_points))
    packs = [sides]
    arrived = [arrived[0]] + [partner(arrived[k], "z", k, depths) for k in range(1, depths)]

    far = planned_features(plan, far_points, token)

    def test(place, *after):
        near, left = prepare(
            place % CORES, packs[place // CORES], [bases[place]], n_domains
        )
        result, _ = tested(far, [near], [left], after)
        tests.append(result)

    tests = []
    test(0)
    mine, token = pick(info, plan, second, arrived)
    packs.append(partner(sides, "z", 1, depths))
    bases.append(sibling(bases[2]))
    tile_owners = jnp.concatenate([side[:, COORDS, :n_tiles] for side in packs]).astype(jnp.int32)
    test(1, token)

    steps = list(range(0, depths, 2))
    held, token = hold([mine] + [partner(mine, "z", k, depths) for k in steps[1:]])
    test(2, token)
    test(3, token)
    pieces = [held] + [partner(held, "group", k, groups) for k in range(1, groups)]
    places = [(k, steps) for k in range(groups)]
    if per % 16:
        half = depths // 2
        sorted_pieces = [[None] * half for _ in range(groups)]
        for piece, (across, steps) in zip(pieces, places):
            for place, along in enumerate(steps):
                sorted_pieces[across][along // 2] = piece[place]
        stacked = jnp.stack([jnp.stack(row) for row in sorted_pieces])
        stacked = stacked[group ^ jnp.arange(groups)][:, (depth // 2) ^ jnp.arange(half)]
        pieces = [stacked.transpose(2, 0, 1, 3, 4).reshape(n_sources, width, cols)]
        places = None
    inverse = preconditioner[0].reshape(-1, cols)

    parts = []
    for column in range(COLUMNS):
        keep, send = gather_products(
            info, tile_owners, tests, pieces, places, depths, n_sources, column
        )
        crossed = sibling(send)
        parts += [keep, crossed[0]]
        for step in reversed(range(1, depths)):
            low = (keep[step] + crossed[step].astype(jnp.float32)).astype(jnp.bfloat16)
            parts.append(partner(low, "z", step, depths))
    return finish(inverse, parts)[None]


def solution(mesh):
    groups, members = mesh.devices.shape
    assert members % SHARE == 0
    fine = Mesh(mesh.devices.reshape(groups, members // CORES, CORES), ("group", "z", "core"))
    every = EVERY
    return jax.shard_map(
        shards,
        mesh=fine,
        in_specs=(
            P(every, None, None),
            P(every, None, None, None),
            P(every, None, None),
            P(every, None, None, None),
            P(every, None, None, None),
            P(every, None, None, None),
            P(),
            P(every, None, None),
        ),
        out_specs=P(every, None, None, None),
        check_vma=False,
    )
```

```python
import functools
import math

import jax
import jax.numpy as jnp
import numpy as np
from jax import lax
from jax.experimental import pallas as pl
from jax.experimental.pallas import tpu as pltpu
from jax.sharding import Mesh
from jax.sharding import PartitionSpec as P

CORES = 2
BLOCK = 256
PIECES = 2
COLUMNS = 2
FEATURES = 32
MIB = 2**20

wire_radius = 0.05
middle = 2.0
green_scale = 1.0 / (4.0 * math.pi)

COS_TERMS = (
    0.9999992215563883,
    -19.738982513245205,
    64.9287265171896,
    -85.27239586454552,
    58.794033467936565,
    -21.076773714433187,
)
SIN_TERMS = (
    6.283055796101308,
    -41.331214171938136,
    81.36681334731878,
    -74.47799414788796,
    32.78138228313484,
)

SHARE = 2 * CORES
COORDS = 3
CHIPS = ("group", "z")
EVERY = ("group", "z", "core")


def dot(left, right):
    return jnp.dot(left, right, preferred_element_type=jnp.float32)


def horner(value, terms):
    total = jnp.float32(terms[-1])
    for term in terms[-2::-1]:
        total = total * value + jnp.float32(term)
    return total


def green_pair(dist_sq):
    inverse = lax.rsqrt(dist_sq)
    distance = dist_sq * inverse
    turn = distance - jnp.round(distance)
    square = turn * turn
    real = horner(square, [green_scale * c for c in COS_TERMS]) * inverse
    imag = horner(square, [-green_scale * c for c in SIN_TERMS]) * (turn * inverse)
    return real.astype(jnp.bfloat16), imag.astype(jnp.bfloat16)


def split_terms(value, count):
    parts = []
    for _ in range(count):
        part = rounded(value)
        parts.append(part)
        value = value - part
    return parts


def point_terms(coords):
    high, low = split_terms(coords.astype(jnp.float32) - middle, 2)
    exact = high + low
    return high, low, jnp.sum(exact * exact, axis=0, keepdims=True)


def rounded(value):
    return value.astype(jnp.bfloat16).astype(jnp.float32)


def near_features(points):
    high, low, norm = point_terms(points)
    one = jnp.ones_like(norm)
    rows = split_terms(norm, 3) + [one, one, one]
    rows += [-2.0 * high, -2.0 * high, -2.0 * low, -2.0 * low]
    used = 6 + 4 * points.shape[0]
    rows.append(jnp.zeros((FEATURES - used, points.shape[1]), jnp.float32))
    return jnp.concatenate(rows, axis=0)


def far_features(points):
    high, low, norm = point_terms(points)
    norm = norm + jnp.float32(wire_radius * wire_radius)
    one = jnp.ones_like(norm)
    rows = [one, one, one] + split_terms(norm, 3)
    rows += [high, low, high, low]
    used = 6 + 4 * points.shape[0]
    rows.append(jnp.zeros((FEATURES - used, points.shape[1]), jnp.float32))
    return jnp.concatenate(rows, axis=0).astype(jnp.bfloat16)


def params(mib):
    return pltpu.CompilerParams(vmem_limit_bytes=mib * MIB)


TOKEN = jax.ShapeDtypeStruct((8, 128), jnp.float32)
SMALL = pl.CostEstimate(flops=1, bytes_accessed=1, transcendentals=0)


def whole(count):
    return [pl.BlockSpec(memory_space=pltpu.VMEM)] * count


def scalars(count):
    return [pl.BlockSpec(memory_space=pltpu.SMEM)] * count


def slot_place(slot, depths, info_ref, plan_ref):
    per_round = plan_ref.shape[1]
    owner = plan_ref[slot // per_round, slot % per_round]
    chip = owner // CORES
    return (chip // depths) ^ info_ref[1], (chip % depths) ^ info_ref[2], (owner % CORES) ^ info_ref[0]


def fold_kernel(core_ref, basis_ref, coeff_ref, keep_ref, send_ref):
    rows, cols = keep_ref.shape
    half = cols // 2
    right = jnp.concatenate([coeff_ref[0], coeff_ref[1]], axis=1)
    for turned, out_ref in ((1, send_ref), (0, keep_ref)):
        first = pl.multiple_of((core_ref[0] ^ turned) * rows, rows)
        upper = dot(basis_ref[0, pl.ds(first, rows)], right)
        lower = dot(basis_ref[1, pl.ds(first, rows)], right)
        out_ref[:, :half] = (upper[:, :half] - lower[:, half:]).astype(jnp.bfloat16)
        out_ref[:, half:] = (upper[:, half:] + lower[:, :half]).astype(jnp.bfloat16)


def fold(core, basis, coeff):
    points, n_basis = basis.shape[1:]
    n_excite = coeff.shape[2]
    shape = jax.ShapeDtypeStruct((points // CORES, 2 * n_excite), jnp.bfloat16)
    return pl.pallas_call(
        fold_kernel,
        in_specs=scalars(1) + whole(2),
        out_specs=whole(2),
        out_shape=[shape, shape],
        compiler_params=params(12),
        cost_estimate=SMALL,
    )(core, basis, coeff)


def pack(points):
    def kernel(*refs):
        *ins, out_ref = refs
        for place, in_ref in enumerate(ins):
            out_ref[place] = in_ref[...]

    return pl.pallas_call(
        kernel,
        out_shape=jax.ShapeDtypeStruct((len(points),) + points[0].shape, points[0].dtype),
        compiler_params=params(4),
        cost_estimate=SMALL,
    )(*points)


def spread(points, chips, depths):
    width = points.shape[1] // SHARE

    def kernel(points_ref, out_ref):
        for device in range(chips * CORES):
            place = (device % CORES) * 2 + (device // CORES) % depths % 2
            out_ref[device] = points_ref[:, place * width : (place + 1) * width]

    return pl.pallas_call(
        kernel,
        out_shape=jax.ShapeDtypeStruct((chips * CORES, points.shape[0], width), points.dtype),
        compiler_params=params(4),
        cost_estimate=SMALL,
    )(points)


def planned_features(plan, points, after):
    n_sources, width = plan.size, points.shape[2]

    def kernel(plan_ref, points_ref, after_ref, out_ref):
        for slot in range(n_sources):
            owner = plan_ref[slot // plan.shape[1], slot % plan.shape[1]]
            out_ref[:, slot * width : (slot + 1) * width] = far_features(points_ref[owner])

    return pl.pallas_call(
        kernel,
        in_specs=scalars(1) + whole(2),
        out_specs=pl.BlockSpec(memory_space=pltpu.VMEM),
        out_shape=jax.ShapeDtypeStruct((FEATURES, n_sources * width), jnp.bfloat16),
        compiler_params=params(4),
        cost_estimate=SMALL,
    )(plan, points, after)


def primary_kernel(depths, info_ref, plan_ref, keep_ref, other_ref, *out_refs):
    core, group, depth = info_ref[0], info_ref[1], info_ref[2]
    first = (group * depths + depth) * CORES
    *out_refs, twin_ref = out_refs
    owners = [plan_ref[i, j] for i in range(plan_ref.shape[0]) for j in range(plan_ref.shape[1])]
    planned = jnp.int32(0)
    twin = jnp.int32(0)
    for place, owner in enumerate(owners):
        planned = planned | (owner == first).astype(jnp.int32)
        for other in owners[:place]:
            twin = twin | (owner // CORES == other // CORES).astype(jnp.int32)
    twin_ref[0] = twin
    own = planned ^ core
    for step, out_ref in enumerate(out_refs):
        for parity in range(2):
            span = slice(parity * (depths // 2), (parity + 1) * (depths // 2))

            @pl.when(own == 1)
            def _():
                out_ref[span] = keep_ref[parity, group ^ step]

            @pl.when(own == 0)
            def _():
                out_ref[span] = other_ref[parity, group ^ step]


def primary_parts(info, plan, depths, keep, other):
    _, count, _, per, cols = keep.shape
    shape = jax.ShapeDtypeStruct((depths, per, cols), keep.dtype)
    return pl.pallas_call(
        functools.partial(primary_kernel, depths),
        in_specs=scalars(2) + whole(2),
        out_specs=whole(count) + scalars(1),
        out_shape=[shape] * count + [jax.ShapeDtypeStruct((1,), jnp.int32)],
        compiler_params=params(6),
        cost_estimate=SMALL,
    )(info, plan, keep, other)


def regroup(info, parts, depths):
    n_groups = len(parts)
    shape = jax.ShapeDtypeStruct((n_groups,) + parts[0].shape[1:], parts[0].dtype)

    def kernel(info_ref, *refs):
        ins, outs, token_ref = refs[:n_groups], refs[n_groups:-1], refs[-1]
        token_ref[...] = jnp.zeros_like(token_ref)
        for step, out_ref in enumerate(outs):
            to = info_ref[2] ^ step
            for place, in_ref in enumerate(ins):
                out_ref[place] = in_ref[(to & 1) * (depths // 2) + (to >> 1)]

    return pl.pallas_call(
        kernel,
        in_specs=scalars(1) + whole(n_groups),
        out_specs=whole(depths + 1),
        out_shape=[shape] * depths + [TOKEN],
        compiler_params=params(6),
        cost_estimate=SMALL,
    )(info, *parts)


def pick(info, plan, second, arrived):
    n_sources, depths = plan.size, len(arrived)
    shape = jax.ShapeDtypeStruct((n_sources,) + arrived[0].shape[1:], arrived[0].dtype)

    def kernel(info_ref, plan_ref, second_ref, *refs):
        *ins, out_ref, token_ref, sem = refs
        token_ref[...] = jnp.zeros_like(token_ref)
        owners = [plan_ref[divmod(slot, plan.shape[1])] for slot in range(n_sources)]
        for slot in range(n_sources):
            across, along, _ = slot_place(slot, depths, info_ref, plan_ref)
            before = jnp.int32(0)
            for owner in owners:
                before = before | (owner == owners[slot] - 1).astype(jnp.int32)
            is_second = (owners[slot] % CORES) * before == 1
            for step, in_ref in enumerate(ins):

                @pl.when((along == step) & jnp.logical_not(is_second))
                def _():
                    out_ref[slot] = in_ref[across]

            @pl.when(is_second)
            def _():
                copy = pltpu.make_async_copy(
                    second_ref.at[owners[slot] // CORES], out_ref.at[slot], sem
                )
                copy.start()
                copy.wait()

    return pl.pallas_call(
        kernel,
        in_specs=scalars(2) + [pl.BlockSpec(memory_space=pl.ANY)] + whole(depths),
        out_specs=whole(2),
        out_shape=[shape, TOKEN],
        scratch_shapes=[pltpu.SemaphoreType.DMA],
        compiler_params=params(6),
        cost_estimate=SMALL,
    )(info, plan, second, *arrived)


def hold(pieces):
    def kernel(*refs):
        *ins, out_ref, token_ref = refs
        token_ref[...] = jnp.zeros_like(token_ref)
        for place, in_ref in enumerate(ins):
            out_ref[place] = in_ref[...]

    shape = jax.ShapeDtypeStruct((len(pieces),) + pieces[0].shape, pieces[0].dtype)
    return pl.pallas_call(
        kernel, out_shape=[shape, TOKEN], compiler_params=params(6), cost_estimate=SMALL
    )(*pieces)


def prepare_kernel(place, points_ref, *refs):
    *basis_refs, near_ref, left_ref = refs
    n_domains = left_ref.shape[0]
    rows = basis_refs[0].shape[1] // n_domains
    n_basis = basis_refs[0].shape[2]
    near_ref[...] = near_features(points_ref[place, :COORDS]).T.astype(jnp.bfloat16)
    for domain in range(n_domains):
        span = slice(domain * rows, (domain + 1) * rows)
        real = basis_refs[0][0, span].T
        imag = basis_refs[-1][basis_refs[-1].shape[0] - 1, span].T
        left_ref[domain, :n_basis, :rows] = real
        left_ref[domain, :n_basis, rows:] = imag
        left_ref[domain, n_basis:, :rows] = -imag
        left_ref[domain, n_basis:, rows:] = real


def prepare(place, points, basis, n_domains):
    _, rows, n_basis = basis[0].shape
    return pl.pallas_call(
        functools.partial(prepare_kernel, place),
        out_shape=[
            jax.ShapeDtypeStruct((rows, FEATURES), jnp.bfloat16),
            jax.ShapeDtypeStruct((n_domains, 2 * n_basis, 2 * rows // n_domains), jnp.bfloat16),
        ],
        compiler_params=params(8),
        cost_estimate=SMALL,
    )(points, *basis)


def tested_kernel(n_devices, n_after, far_ref, *refs):
    refs = refs[n_after:]
    nears, lefts, outs = (refs[i * n_devices : (i + 1) * n_devices] for i in range(3))
    token_ref, *green = refs[3 * n_devices :]
    token_ref[...] = jnp.zeros_like(token_ref)
    n_domains, size, _ = lefts[0].shape
    rows = nears[0].shape[0] // n_domains
    n_basis = size // 2
    blocks = far_ref.shape[1] // BLOCK
    work = [(i, d, b) for i in range(n_devices) for d in range(n_domains) for b in range(blocks)]

    def interact(index, piece):
        device, domain, block = work[index]
        part = rows // PIECES // 4
        span = slice(block * BLOCK, (block + 1) * BLOCK)
        into = green[index % 2]
        for first in range(4 * piece * part, 4 * (piece + 1) * part, part):
            near = nears[device][domain * rows + first : domain * rows + first + part]
            real, imag = green_pair(dot(near, far_ref[:, span]))
            into[first : first + part] = real
            into[rows + first : rows + first + part] = imag

    def test(index, piece):
        device, domain, block = work[index]
        start = (PIECES * block + piece) * BLOCK
        some = slice(piece * n_basis, (piece + 1) * n_basis)
        result = dot(lefts[device][domain, some], green[index % 2][...])
        outs[device][domain, :, start : start + BLOCK] = result.astype(jnp.bfloat16)

    for piece in range(PIECES):
        interact(0, piece)
    for index in range(len(work)):
        for piece in range(PIECES):
            test(index, piece)
            if index + 1 < len(work):
                interact(index + 1, piece)


def tested(far, nears, lefts, after):
    n_domains, size, twice = lefts[0].shape
    columns = far.shape[1]
    shape = jax.ShapeDtypeStruct((n_domains, size // 2, 2 * columns), jnp.bfloat16)
    return pl.pallas_call(
        functools.partial(tested_kernel, len(nears), len(after)),
        out_shape=[shape] * len(nears) + [TOKEN],
        scratch_shapes=[
            pltpu.VMEM((twice, BLOCK), jnp.bfloat16),
            pltpu.VMEM((twice, BLOCK), jnp.bfloat16),
        ],
        compiler_params=params(8),
        cost_estimate=pl.CostEstimate(
            flops=8 * len(nears) * n_domains * size * twice * columns,
            bytes_accessed=4 * MIB,
            transcendentals=0,
        ),
    )(far, *after, *nears, *lefts)


def gather_kernel(n_tests, places, column, info_ref, *refs):
    owner_ref, tests = refs[0], refs[1 : n_tests + 1]
    *pieces, keep_ref, send_ref, far, total = refs[n_tests + 1 :]
    n_sources, twice, cols = far.shape
    width, half = twice // 2, cols // 2
    n_depth, n_basis, _ = keep_ref.shape
    n_domains = tests[0].shape[0]
    core, group, depth = info_ref[0], info_ref[1], info_ref[2]

    def fill(start, per, value):
        for slot in range(n_sources):
            block = value(slot)
            real = block[:, column * half : (column + 1) * half]
            imag = block[:, (COLUMNS + column) * half : (COLUMNS + column + 1) * half]
            far[slot, pl.ds(start, per), :half] = real
            far[slot, pl.ds(start, per), half:] = imag
            far[slot, pl.ds(width + start, per), :half] = -imag
            far[slot, pl.ds(width + start, per), half:] = real

    if places is None:
        fill(0, width, lambda slot: pieces[0][slot])
    else:
        for piece, (across, steps) in zip(pieces, places):
            per = piece.shape[-2]
            for place, along in enumerate(steps):
                chip = (group ^ across) * (n_depth // 2) + ((depth ^ along) >> 1)
                start = pl.multiple_of(chip * per, per)
                fill(start, per, lambda slot: piece[place, slot])
    total[...] = jnp.zeros_like(total)

    def add_domain(domain, carry):
        for place, test in enumerate(tests):
            for slot in range(n_sources):
                left = test[domain, :, slot * twice : (slot + 1) * twice]
                owner = owner_ref[place, domain * n_sources + slot]
                total[owner] += dot(left, far[slot])
        return carry

    lax.fori_loop(0, n_domains, add_domain, 0)
    for step in range(n_depth):
        owner = CORES * (depth ^ step) + core
        keep_ref[step] = total[owner]
        send_ref[step] = total[owner ^ 1].astype(jnp.bfloat16)


def gather_products(info, owners, tests, pieces, places, depths, n_sources, column):
    n_domains, n_basis, columns = tests[0].shape
    cols = pieces[0].shape[-1] // COLUMNS
    shape = (depths, n_basis, cols)
    return pl.pallas_call(
        functools.partial(gather_kernel, len(tests), places, column),
        in_specs=scalars(2) + whole(len(tests) + len(pieces)),
        out_specs=whole(2),
        out_shape=[
            jax.ShapeDtypeStruct(shape, jnp.float32),
            jax.ShapeDtypeStruct(shape, jnp.bfloat16),
        ],
        scratch_shapes=[
            pltpu.VMEM((n_sources, columns // n_sources, cols), jnp.bfloat16),
            pltpu.VMEM((CORES * depths, n_basis, cols), jnp.float32),
        ],
        compiler_params=params(14),
        cost_estimate=pl.CostEstimate(
            flops=2 * len(tests) * n_domains * n_basis * columns * cols,
            bytes_accessed=MIB,
            transcendentals=0,
        ),
    )(info, owners, *tests, *pieces)


def finish_kernel(inverse_ref, *refs):
    *parts, out_ref = refs
    count = len(parts) // COLUMNS
    for column in range(COLUMNS):
        own_ref, *others = parts[column * count : (column + 1) * count]
        half = own_ref.shape[1] // 2
        summed = own_ref[...]
        for other in others:
            summed = summed + other[...].astype(jnp.float32)
        low = summed.astype(jnp.bfloat16)
        upper = dot(inverse_ref[:, : low.shape[0]], low)
        lower = dot(inverse_ref[:, low.shape[0] :], low)
        span = slice(column * half, (column + 1) * half)
        out_ref[:, 0, span] = upper[:, :half] - lower[:, half:]
        out_ref[:, 1, span] = upper[:, half:] + lower[:, :half]


def finish(inverse, parts):
    rows, cols = inverse.shape
    return pl.pallas_call(
        finish_kernel,
        out_shape=jax.ShapeDtypeStruct((rows, 2, cols // 2), jnp.float32),
        compiler_params=params(12),
    )(inverse, *parts)


def partner(value, axis, step, size):
    return lax.ppermute(value, axis, [(i, i ^ step) for i in range(size)])


def shards(
    test_points,
    test_basis,
    source_points,
    source_basis,
    excitation,
    preconditioner,
    plan,
    solver_owner,
):
    groups, depths = lax.axis_size("group"), lax.axis_size("z")
    group, depth, core = lax.axis_index("group"), lax.axis_index("z"), lax.axis_index("core")
    chips = groups * depths
    n_domains, n_sources = solver_owner.shape[1:]
    src_points = source_points.shape[2]
    n_excite = excitation.shape[3]
    width = src_points // SHARE
    per = CORES * width // chips
    cols = 2 * n_excite
    info = jnp.stack([core, group, depth, depths]).astype(jnp.int32)
    def sibling(value):
        return partner(value, "core", 1, CORES)

    bases = [test_basis[0], sibling(test_basis[0]), partner(test_basis[0], "z", 1, depths)]

    keep, send = fold(info, source_basis[0], excitation[0])
    other = sibling(send)
    cut = (2, groups, depths // 2, per, cols)
    *parts, twin = primary_parts(info, plan, depths, keep.reshape(cut), other.reshape(cut))

    def rest_of_second(keep, other):
        first_planned = jnp.any(plan == (group * depths + depth) * CORES)
        rest = jnp.where(first_planned == (core == 0), other, keep).reshape(cut)
        rest = rest.transpose(1, 2, 0, 3, 4).reshape(chips, per, cols)
        return lax.all_to_all(rest, CHIPS, 0, 0, tiled=True)

    second = lax.cond(
        twin[0] > 0, rest_of_second, lambda _, other: other.reshape(chips, per, cols), keep, other
    )
    parts, source_points, test_points, solver_owner = lax.optimization_barrier(
        (parts, source_points, test_points, solver_owner)
    )
    parts = [parts[0]] + [partner(parts[k], "group", k, groups) for k in range(1, groups)]

    far_points = lax.all_to_all(spread(source_points[0], chips, depths), EVERY, 0, 0, tiled=True)
    n_tiles = n_domains * n_sources
    owner_row = solver_owner[0].reshape(1, n_tiles).astype(test_points.dtype)
    owner_row = jnp.pad(owner_row, ((0, 0), (0, src_points - n_tiles)))
    sides = jnp.concatenate([test_points[0], owner_row], axis=0)
    sides = pack((sides, sibling(sides)))

    parts, bases, sides = lax.optimization_barrier((parts, bases, sides))
    *arrived, token = regroup(info, parts, depths)
    token, far_points = lax.optimization_barrier((token, far_points))
    packs = [sides]
    arrived = [arrived[0]] + [partner(arrived[k], "z", k, depths) for k in range(1, depths)]

    far = planned_features(plan, far_points, token)

    def test(place, *after):
        near, left = prepare(
            place % CORES, packs[place // CORES], [bases[place]], n_domains
        )
        result, _ = tested(far, [near], [left], after)
        tests.append(result)

    tests = []
    test(0)
    mine, token = pick(info, plan, second, arrived)
    packs.append(partner(sides, "z", 1, depths))
    bases.append(sibling(bases[2]))
    tile_owners = jnp.concatenate([side[:, COORDS, :n_tiles] for side in packs]).astype(jnp.int32)
    test(1, token)

    steps = list(range(0, depths, 2))
    held, token = hold([mine] + [partner(mine, "z", k, depths) for k in steps[1:]])
    test(2, token)
    test(3, token)
    pieces = [held] + [partner(held, "group", k, groups) for k in range(1, groups)]
    places = [(k, steps) for k in range(groups)]
    if per % 16:
        half = depths // 2
        sorted_pieces = [[None] * half for _ in range(groups)]
        for piece, (across, steps) in zip(pieces, places):
            for place, along in enumerate(steps):
                sorted_pieces[across][along // 2] = piece[place]
        stacked = jnp.stack([jnp.stack(row) for row in sorted_pieces])
        stacked = stacked[group ^ jnp.arange(groups)][:, (depth // 2) ^ jnp.arange(half)]
        pieces = [stacked.transpose(2, 0, 1, 3, 4).reshape(n_sources, width, cols)]
        places = None
    inverse = preconditioner[0].reshape(-1, cols)

    parts = []
    for column in range(COLUMNS):
        keep, send = gather_products(
            info, tile_owners, tests, pieces, places, depths, n_sources, column
        )
        crossed = sibling(send)
        total = keep + crossed.astype(jnp.float32)
        parts.append(total[0])
        for step in reversed(range(1, depths)):
            low = total[step].astype(jnp.bfloat16)
            parts.append(partner(low, "z", step, depths))
    return finish(inverse, parts)[None]


def solution(mesh):
    groups, members = mesh.devices.shape
    assert members % SHARE == 0
    fine = Mesh(mesh.devices.reshape(groups, members // CORES, CORES), ("group", "z", "core"))
    every = EVERY
    return jax.shard_map(
        shards,
        mesh=fine,
        in_specs=(
            P(every, None, None),
            P(every, None, None, None),
            P(every, None, None),
            P(every, None, None, None),
            P(every, None, None, None),
            P(every, None, None, None),
            P(),
            P(every, None, None),
        ),
        out_specs=P(every, None, None, None),
        check_vma=False,
    )
```
